256 devices in a mesh: rep: 16 (over y, z_lo, core), exp: 16 (over x, z_hi).
Axes of the slice: x: 4, y: 4, z: 8 (z_hi: 4, z_lo: 2; z = z_hi * 2 + z_lo), core: 2. Of those that a mesh axis runs over, the one named last changes fastest.
Arguments:
- tokens: bfloat16 [32768, 1440], P(('rep', 'exp')), may hold values from -6 to 6
- expert_ids: int32 [32768, 4], P(('rep', 'exp')), may hold values from 0 to 127, all different within a row; in each aligned block of 128 rows (0 to 127, 128 to 255, ...) at most 5 rows name the same one
- route_weights: float32 [32768, 4], P(('rep', 'exp')), may hold values from 0.05 to 1
- w_in: bfloat16 [16, 16, 1440, 1440], P('rep', 'exp'), may hold values from -0.15625 to 0.15625
- w_down: bfloat16 [16, 16, 720, 1440], P('rep', 'exp'), may hold values from -0.15625 to 0.15625
- spare_source: int32 [2], replicated, may hold values from 0 to 7, as said below
- spare_host: int32 [2], replicated, may hold values from 8 to 15, as said below
Outputs:
- mixed: bfloat16 [32768, 1440], P(('rep', 'exp'))
- slot_load: int32 [16, 16], P('rep', 'exp')
The draws below stay inside these ranges and needn't reach their ends.
Inputs may be any that keep to these rules, and one draw needn't show every extreme that they name: `expert_ids`: in the 128 rows of one device no expert is named more than 5 times, a bound that some block reaches. `spare_source`: 2 different exp indices of the lower half of the exp axis. `spare_host`: 2 different exp indices of the upper half of the exp axis.
All inputs are finite; a program needn't handle non-finite values.
Results may differ from the reference program's by a relative error of at most 0.0058.
Values may be sent and summed in bfloat16 or wider, within the bound.
A program may use at most 128 MiB of HBM per device.

```python
import math
import jax
import jax.numpy as jnp
import numpy as np
from jax import lax

D = 1440
FF = 1440
TOPK = 4
HOT = 2
TOK_DEV = 128
E = 128
FF_HALF = 720
CAP = 5
TOKENS = 32768
N_REP = 16
N_EXP = 16


def pick_columns(key, offset):
    middle = N_EXP // 2
    others = jax.random.permutation(key, jnp.arange(middle - 1, dtype=jnp.int32))[:HOT - 1]
    picked = jnp.concatenate([jnp.full((1,), middle - 1, jnp.int32), others])
    picked = jax.random.permutation(jax.random.fold_in(key, 5), picked)
    return (picked + offset).astype(jnp.int32)


def draw_spare_source(key, part):
    key = jax.random.fold_in(key, 11)
    return pick_columns(key, 0)


def draw_spare_host(key, part):
    key = jax.random.fold_in(key, 12)
    return pick_columns(key, N_EXP // 2)


def level_of(own_key, shape, split, smallest, top_value):
    factor_of, own = 1.0, jax.random.fold_in(own_key, 6)
    for axis_at, parts in split:
        steps = jnp.exp(jax.random.uniform(jax.random.fold_in(own, axis_at), (parts,), jnp.float32, smallest / len(split), top_value / len(split)))
        factor_of = factor_of * jnp.repeat(steps, shape[axis_at] // parts).reshape([-1 if axis == axis_at else 1 for axis in range(len(shape))])
    return factor_of


def deal_out(stream_key, own, number, rows, number_of, top, bound, skew):
    ranking = jax.random.permutation(stream_key, number_of)
    packed, common = portions_of(number_of, rows * top, bound, skew, True), portions_of(number_of, rows * top, bound, skew, False)
    places = jnp.arange(number_of)

    def named(sizes, offset_by):
        used = int((sizes > 0).sum())
        fixed = max(1, used // 4)
        shifted = fixed + (places - fixed + offset_by * (used - fixed)) % max(1, number_of - fixed)
        return jnp.zeros((number_of,), jnp.int32).at[ranking[jnp.where(places < fixed, places, shifted)]].set(jnp.asarray(sizes, jnp.int32))

    sizes = jnp.where(number % 4 == 0, named(packed, number // 4), named(common, number - number // 4 - 1))
    mixed = jax.random.permutation(jax.random.fold_in(own, 3), number_of)
    donor, taker = mixed[0:number_of // 2 * 2:2], mixed[1:number_of // 2 * 2:2]
    margin = jnp.minimum(sizes[donor] - 1, bound - sizes[taker]) // 2
    margin = jnp.where((donor == ranking[0]) | (taker == ranking[0]) | (sizes[taker] == 0), 0, jnp.maximum(margin, 0))
    shifted = jax.random.randint(jax.random.fold_in(own, 4), (number_of // 2,), 0, 1 << 20) % (margin + 1)
    sizes = sizes.at[donor].add(-shifted).at[taker].add(shifted)
    items = jnp.searchsorted(jnp.cumsum(sizes), jnp.arange(rows * top), side="right").astype(jnp.int32)
    grid = items.reshape(top, rows).T
    grid = grid[jax.random.permutation(jax.random.fold_in(own, 1), rows)]
    offset_by = jax.random.randint(jax.random.fold_in(own, 2), (rows, 1), 0, top)
    return jnp.take_along_axis(grid, (jnp.arange(top)[None, :] + offset_by) % top, axis=1)


def portions_of(count, total, most, skew, full):
    weights = [(1 << 20) // math.isqrt(rank ** skew) + 1 for rank in range(1, count + 1)]
    largest = most if full else min(most, max(-(-total // count), total * weights[0] // sum(weights)))
    least = 1 if total - largest >= count - 1 else 0
    given, rest = [largest] + [least] * (count - 1), total - largest - least * (count - 1)
    while rest > 0:
        free = [i for i in range(1, count) if given[i] < largest] or [i for i in range(1, count) if given[i] < most]
        pool, left = sum([weights[i] for i in free]), rest
        for i in free:
            addition = min(most - given[i], max(1, left * weights[i] // pool), rest)
            given[i] = given[i] + addition
            rest = rest - addition
    return np.array(given)


def normal_values(stream_key, extent, spread, limit, shards=(), held_as=jnp.bfloat16):
    array = spread * jax.random.normal(stream_key, extent, jnp.float32)
    if shards:
        array = array * level_of(stream_key, extent, shards, -0.22, 0.18)
    return jnp.clip(array, -limit, limit).astype(held_as)


def setup_inputs(seed: int = 0) -> dict:
    splits = jax.random.split(jax.random.key(seed), 8)
    tokens = normal_values(splits[0], (TOKENS, D), 1.0, 6.0, ((0, 256),))
    expert_ids_keys = jax.random.split(jax.random.fold_in(splits[1], 1), TOKENS // TOK_DEV)
    expert_ids_turns = jax.random.permutation(jax.random.fold_in(splits[1], 3), TOKENS // TOK_DEV)
    expert_ids = jax.vmap(lambda own, number: deal_out(jax.random.fold_in(splits[1], 2), own, number, TOK_DEV, E, TOPK, CAP, 2))(expert_ids_keys, expert_ids_turns).reshape((TOKENS, TOPK))
    route_weights = jnp.clip(jnp.exp(math.log(1.0) - 2.9957323 * jax.random.uniform(splits[2], (TOKENS, TOPK), jnp.float32) ** level_of(splits[2], (TOKENS, TOPK), ((0, 256),), -0.2, 0.2)), 0.05, 1.0)
    w_in = normal_values(splits[3], (N_REP, N_EXP, D, 2 * FF_HALF), D ** -0.5, 0.15625, ((0, 16), (1, 16)))
    w_down = normal_values(splits[4], (N_REP, N_EXP, FF_HALF, D), FF ** -0.5, 0.15625, ((0, 16), (1, 16)))
    spare_source = draw_spare_source(jax.random.fold_in(splits[7], 71), 0)
    spare_host = draw_spare_host(jax.random.fold_in(splits[7], 71), 0)
    return {"tokens": tokens, "expert_ids": expert_ids, "route_weights": route_weights, "w_in": w_in, "w_down": w_down, "spare_source": spare_source, "spare_host": spare_host}


def expert_half(gathered, weight_in, weight_down):
    projected = jnp.dot(gathered, weight_in, preferred_element_type=jnp.float32)
    half_width = weight_down.shape[0]
    gate_part = projected[:, :half_width]
    up_part = projected[:, half_width:]
    hidden = ((up_part + 1.0) * gate_part * jax.nn.sigmoid(1.702 * gate_part)).astype(jnp.bfloat16)
    return jnp.dot(hidden, weight_down, preferred_element_type=jnp.float32).astype(jnp.bfloat16)


def reference(tokens, expert_ids, route_weights, w_in, w_down, spare_source, spare_host):
    group_count = N_REP // 2
    device_count = N_REP * N_EXP
    expert_count = group_count * N_EXP
    per_device = TOK_DEV * TOPK
    chosen = expert_ids.reshape(device_count, per_device)
    one_hot = (chosen[:, :, None] == jnp.arange(expert_count, dtype=jnp.int32)[None, None, :]).astype(jnp.int32)
    order_rank = jnp.sum(jnp.cumsum(one_hot, axis=1) * one_hot, axis=2) - 1
    device_of = jnp.broadcast_to(jnp.arange(device_count, dtype=jnp.int32)[:, None], chosen.shape)
    token_of = (jnp.arange(device_count * per_device, dtype=jnp.int32) // TOPK).reshape(device_count, per_device)
    slot_token = jnp.full((expert_count, device_count, CAP), TOKENS, jnp.int32)
    slot_token = slot_token.at[chosen, device_of, order_rank].set(token_of)
    slot_weight = jnp.zeros((expert_count, device_count, CAP), jnp.float32)
    slot_weight = slot_weight.at[chosen, device_of, order_rank].set(route_weights.reshape(device_count, per_device))
    padded = jnp.concatenate([tokens, jnp.zeros((1, tokens.shape[1]), jnp.bfloat16)], axis=0)

    def one_expert(carry, expert):
        residue = expert % group_count
        home = expert // group_count
        picked = slot_token[expert].reshape(-1)
        weights = slot_weight[expert].reshape(-1)
        gathered = padded[picked]
        first = expert_half(gathered, w_in[residue, home], w_down[residue, home])
        second = expert_half(gathered, w_in[group_count + residue, home], w_down[group_count + residue, home])
        summed = first.astype(jnp.float32) + second.astype(jnp.float32)
        carry = carry.at[picked].add(weights[:, None] * summed)
        return carry, None

    start = jnp.zeros((TOKENS + 1, tokens.shape[1]), jnp.float32)
    result, _ = lax.scan(one_expert, start, jnp.arange(expert_count, dtype=jnp.int32))
    mixed = result[:TOKENS].astype(jnp.bfloat16)

    counts = jnp.sum(one_hot, axis=1).reshape(N_REP, N_EXP, expert_count)
    overall = jnp.sum(counts, axis=(0, 1))
    upper_sum = jnp.sum(counts[group_count:], axis=(0, 1))
    residues = jnp.arange(N_REP, dtype=jnp.int32) % group_count
    column_ids = jnp.arange(N_EXP, dtype=jnp.int32)
    own_expert = column_ids[None, :] * group_count + residues[:, None]
    is_source = jnp.any(column_ids[:, None] == spare_source[None, :], axis=1)
    slot_load = overall[own_expert] - jnp.where(is_source[None, :], upper_sum[own_expert], 0)
    for index_hot in range(HOT):
        copied = upper_sum[spare_source[index_hot] * group_count + residues]
        slot_load = slot_load + jnp.where((column_ids == spare_host[index_hot])[None, :], copied[:, None], 0)
    return mixed, slot_load.astype(jnp.int32)
```

```python
import jax
import jax.numpy as jnp
from jax import lax
from jax.experimental import pallas as pl
from jax.experimental.pallas import tpu as pltpu
from jax.sharding import PartitionSpec as P

MESH = pl.DeviceIdType.MESH
F32 = jnp.float32
BF16 = jnp.bfloat16

NX, NY, NZ = 4, 4, 8
NSRC = 2 * NZ
CAP = 5
UNIT = NSRC * CAP
ROWS = NX * 2 * UNIT
CODE = 1024
CHUNKS = ((0, 512), (512, 1024), (1024, 1440))
NC = len(CHUNKS)
OFFS = (0, -1, 1, -2, 2, -3, 3, 4)


def device(x, y, z, k):
    return (y * 4 + lax.rem(z, 2) * 2 + k, x * 4 + lax.div(z, 2))


def moe_kernel(ids_ref, wts_ref, tok_ref, wi_hbm, wd_hbm, out_ref, *scratch):
    T, G, XY, PP, RY, SS, RX, ZC, ZR = (scratch[i * NC:(i + 1) * NC] for i in range(9))
    meta, OH, CT, WI, WU, WD, send_sems, recv_sems, meta_send, meta_recv, load_sems = scratch[9 * NC:]
    tok_rows = tok_ref.shape[0]
    half = tok_rows // 2
    ff = WD.shape[0]

    rep, ex = lax.axis_index("rep"), lax.axis_index("exp")
    y, k = lax.div(rep, 4), lax.rem(rep, 2)
    x = lax.div(ex, 4)
    z = lax.rem(ex, 4) * 2 + lax.rem(lax.div(rep, 2), 2)
    me = z * 2 + k
    p = lax.rem(y, 2)

    def zat(d):
        return lax.rem(z + d + NZ, NZ)

    def yat(d):
        return lax.rem(y + d + NY, NY)

    def xat(d):
        return lax.rem(x + d + NX, NX)

    ids_of = {}
    sends = []

    def sem_of(name):
        if name not in ids_of:
            ids_of[name] = len(ids_of)
        return ids_of[name]

    def send(name, src, dst, to):
        i = sem_of(name)
        copy = pltpu.make_async_remote_copy(
            src_ref=src, dst_ref=dst, send_sem=send_sems.at[i], recv_sem=recv_sems.at[i],
            device_id=to, device_id_type=MESH)
        copy.start()
        sends.append(copy)

    def arrived(name, dst):
        i = sem_of(name)
        pltpu.make_async_remote_copy(
            src_ref=dst, dst_ref=dst, send_sem=send_sems.at[i], recv_sem=recv_sems.at[i],
            device_id=device(x, y, z, 1 - k), device_id_type=MESH).wait_recv()

    def drain():
        for copy in sends:
            copy.wait_send()
        sends.clear()

    barrier = pltpu.get_barrier_semaphore()
    for j in range(1, NSRC):
        peer = lax.rem(me + j, NSRC)
        pl.semaphore_signal(barrier, inc=1, device_id=device(x, y, lax.div(peer, 2), lax.rem(peer, 2)), device_id_type=MESH)
    for j in range(1, NX):
        pl.semaphore_signal(barrier, inc=1, device_id=device(xat(j), y, z, k), device_id_type=MESH)
    for j in range(1, NY):
        pl.semaphore_signal(barrier, inc=1, device_id=device(x, yat(j), z, k), device_id_type=MESH)

    load_in = pltpu.make_async_copy(wi_hbm, WI, load_sems.at[0])
    load_down = pltpu.make_async_copy(wd_hbm, WD, load_sems.at[1])
    load_in.start()
    load_down.start()
    for c, (lo, hi) in enumerate(CHUNKS):
        T[c][me] = tok_ref[:, lo:hi]
    pl.semaphore_wait(barrier, NSRC - 1 + NX - 1 + NY - 1)

    def block(c, d, rows=None, core=None):
        ref = T[c].at[zat(d) * 2 + (k if core is None else core)]
        return ref if rows is None else ref.at[pl.ds(rows, half)]

    def to_sibling(c, d):
        send(("sib", c, d), block(c, d), block(c, d), device(x, y, z, 1 - k))

    def gather_step(c, s):
        if s == 1:
            to_send = ((1, block(c, 0)), (-1, block(c, 0)))
        else:
            for way in (1, -1):
                rows = None if s <= 4 else (0 if way == 1 else half)
                arrived(("ag", c, s - 1, way), block(c, -(s - 1) * way, rows))
            to_send = ()
            if s <= 4:
                to_send = tuple(
                    (way, block(c, -(s - 1) * way, None if s < 4 else (0 if way == 1 else half))) for way in (1, -1))
        for way, ref in to_send:
            send(("ag", c, s, way), ref, ref, device(x, y, zat(way), k))
        if s == 1:
            to_sibling(c, 0)
        elif s <= 4:
            to_sibling(c, -(s - 1))
            to_sibling(c, s - 1)
        else:
            to_sibling(c, 4)

    def make_meta():
        experts = lax.broadcasted_iota(jnp.int32, (tok_rows, 128), 1)
        total = jnp.zeros((tok_rows, 128), F32)
        hits = []
        for i in range(4):
            hit = (ids_ref[:, i:i + 1] == experts).astype(F32)
            hits.append(hit)
            total = total + hit
        before = (lax.broadcasted_iota(jnp.int32, (tok_rows, tok_rows), 0)
                  > lax.broadcasted_iota(jnp.int32, (tok_rows, tok_rows), 1)).astype(BF16)
        earlier = jnp.dot(before, total.astype(BF16), preferred_element_type=F32)
        table = jnp.zeros((tok_rows, 128), F32)
        for i in range(4):
            rank = jnp.sum(earlier * hits[i], axis=1, keepdims=True)
            e = ids_ref[:, i:i + 1]
            owner = ((e >> 3) & 3) * 4 + ((e >> 1) & 1) * 2 + (e & 1)
            place = ((e >> 5) * 2 + ((e >> 2) & 1)) * UNIT
            code = (owner * CODE + place).astype(F32) + rank
            table = jnp.where(experts == i, code, table)
            table = jnp.where(experts == 4 + i, wts_ref[:, i:i + 1], table)
        meta[me] = table.T[0:8, :]

    def send_meta():
        def one(j, carry):
            peer = lax.rem(me + j, NSRC)
            pltpu.make_async_remote_copy(
                src_ref=meta.at[me], dst_ref=meta.at[me], send_sem=meta_send.at[j], recv_sem=meta_recv.at[j],
                device_id=device(x, y, lax.div(peer, 2), lax.rem(peer, 2)), device_id_type=MESH).start()
            return carry
        lax.fori_loop(1, NSRC, one, 0)

    def meta_copy(j):
        peer = lax.rem(me + NSRC - j, NSRC)
        return pltpu.make_async_remote_copy(
            src_ref=meta.at[peer], dst_ref=meta.at[peer], send_sem=meta_send.at[j], recv_sem=meta_recv.at[j],
            device_id=device(x, y, lax.div(peer, 2), lax.rem(peer, 2)), device_id_type=MESH)

    def build_pick():
        def wait_one(j, carry):
            meta_copy(j).wait_recv()
            return carry
        lax.fori_loop(1, NSRC, wait_one, 0)

        def one(s, carry):
            row = lax.broadcasted_iota(jnp.int32, (ROWS, tok_rows), 0).astype(F32)
            shift = (s * CAP - me * CODE).astype(F32)
            codes = meta[s] + shift
            hit = row == codes[0:1, :]
            for i in range(1, 4):
                hit = jnp.logical_or(hit, row == codes[i:i + 1, :])
            OH[:, pl.ds(pl.multiple_of(s * tok_rows, tok_rows), tok_rows)] = jnp.where(hit, 1.0, 0.0).astype(BF16)
            return carry
        lax.fori_loop(0, NSRC, one, 0)

    def build_combine():
        def one(s, carry):
            col = lax.broadcasted_iota(jnp.int32, (tok_rows, ROWS), 1).astype(F32)
            shift = (s * CAP - me * CODE).astype(F32)
            info = meta[s].T
            total = jnp.zeros((tok_rows, ROWS), F32)
            for i in range(4):
                total = jnp.where(col == info[:, i:i + 1] + shift, info[:, 4 + i:5 + i], total)
            CT[pl.ds(pl.multiple_of(s * tok_rows, tok_rows), tok_rows), :] = total.astype(BF16)
            return carry
        lax.fori_loop(0, NSRC, one, 0)

    def x_stage(c):
        width = CHUNKS[c][1] - CHUNKS[c][0]
        for d in OFFS:
            arrived(("sib", c, d), block(c, d, core=1 - k))
        for j in (2, 1, 3, 0):
            xp = xat(j)
            picked = jnp.dot(
                OH[pl.ds(pl.multiple_of(xp * 2 * UNIT, 2 * UNIT), 2 * UNIT), :],
                T[c][...].reshape(NSRC * tok_rows, width),
                preferred_element_type=F32).astype(BF16).reshape(2, UNIT, width)
            if j == 0:
                XY[c][0, x] = picked[0]
                XY[c][1, x] = picked[1]
            else:
                G[c][j - 1] = picked
                send(("x", c, j), G[c].at[j - 1], XY[c].at[pl.ds(0, 2), x], device(xp, y, z, k))

    def y_stage(c):
        for j in (1, 3, 2):
            arrived(("x", c, j), XY[c].at[pl.ds(0, 2), xat(-j)])
        for j in (1, 3, 2):
            a = lax.rem(p + j, 2)
            send(("y", c, j), XY[c].at[a], XY[c].at[1 + j], device(x, yat(j), z, k))

    def load_weights():
        load_in.wait()
        load_down.wait()

        def one(i, carry):
            rows = pl.ds(pl.multiple_of(i * 160, 16), 160)
            WU[rows, :] = WI[rows, ff:2 * ff]
            return carry
        lax.fori_loop(0, WI.shape[0] // 160, one, 0)

    def expert(j):
        slot = p if j == 0 else 1 + j
        if j:
            for c in range(NC):
                arrived(("y", c, j), XY[c].at[slot])

        def one(q, carry):
            gate = up = None
            for c, (lo, hi) in enumerate(CHUNKS):
                rows = XY[c][slot, pl.ds(q * 2, 2)].reshape(2 * UNIT, hi - lo)
                g = jnp.dot(rows, WI[lo:hi, 0:ff], preferred_element_type=F32)
                u = jnp.dot(rows, WU[lo:hi, :], preferred_element_type=F32)
                gate, up = (g, u) if gate is None else (gate + g, up + u)
            hidden = ((up + 1.0) * gate * jax.nn.sigmoid(1.702 * gate)).astype(BF16)
            for c, (lo, hi) in enumerate(CHUNKS):
                part = jnp.dot(hidden, WD[:, lo:hi], preferred_element_type=F32).astype(BF16)
                PP[c][j, pl.ds(q * 2, 2)] = part.reshape(2, UNIT, hi - lo)
            return carry
        lax.fori_loop(0, 2, one, 0)
        if j:
            for c in range(NC):
                send(("ry", c, j), PP[c].at[j], RY[c].at[j - 1], device(x, yat(-j), z, k))

    def halves(c, odd):
        if odd:
            arrived(("ry", c, 1), RY[c].at[0])
            arrived(("ry", c, 3), RY[c].at[2])
            first, second = RY[c].at[0], RY[c].at[2]
        else:
            arrived(("ry", c, 2), RY[c].at[1])
            first, second = PP[c].at[0], RY[c].at[1]
        a = lax.rem(p + odd, 2)

        def one(i, carry):
            SS[c][odd, i] = (first[i].astype(F32) + second[i].astype(F32)).astype(BF16)
            return carry
        lax.fori_loop(0, NX, one, 0)
        for j in (2, 1, 3):
            xs = xat(j)
            send(("rx", c, odd, j), SS[c].at[odd, xs], RX[c].at[x, a], device(xs, y, z, k))
        RX[c][x, a] = SS[c][odd, x]

    def combined(c, s):
        width = CHUNKS[c][1] - CHUNKS[c][0]
        return jnp.dot(
            CT[pl.ds(pl.multiple_of(s * tok_rows, tok_rows), tok_rows), :],
            RX[c][...].reshape(ROWS, width), preferred_element_type=F32)

    def combine_sibling(c):
        for odd in (1, 0):
            a = lax.rem(p + odd, 2)
            for j in (2, 1, 3):
                arrived(("rx", c, odd, j), RX[c].at[xat(-j), a])
        for d in OFFS[::-1]:
            s = zat(d) * 2 + 1 - k
            T[c][s] = combined(c, s).astype(BF16)
            send(("zc", c, d), T[c].at[s], ZC[c].at[zat(d)], device(x, y, z, 1 - k))

    def scatter_step(c, s):
        lo, hi = CHUNKS[c]
        if s == 0:
            arrived(("zc", c, 4), ZC[c].at[zat(4)])
            own = T[c].at[zat(4) * 2 + k]
            own[...] = (combined(c, zat(4) * 2 + k) + ZC[c][zat(4)].astype(F32)).astype(BF16)
            for i, way in enumerate((1, -1)):
                rows = pl.ds(i * half, half)
                send(("rs", c, 0, way), own.at[rows], ZR[c].at[i * 4, rows], device(x, y, zat(way), k))
        elif s < 4:
            for i, way in enumerate((1, -1)):
                d = way * (4 - s)
                arrived(("zc", c, d), ZC[c].at[zat(d)])
                total = combined(c, zat(d) * 2 + k) + ZC[c][zat(d)].astype(F32)
                own = T[c].at[zat(d) * 2 + k]
                if s == 1:
                    rows = pl.ds(i * half, half)
                    arrived(("rs", c, 0, way), ZR[c].at[i * 4, rows])
                    mine = total[i * half:(i + 1) * half] + ZR[c][i * 4, rows].astype(F32)
                    own[rows, :] = mine.astype(BF16)
                    other = 1 - i
                    own[pl.ds(other * half, half), :] = total[other * half:(other + 1) * half].astype(BF16)
                else:
                    arrived(("rs", c, s - 1, way), ZR[c].at[i * 4 + s - 1])
                    own[...] = (total + ZR[c][i * 4 + s - 1].astype(F32)).astype(BF16)
                send(("rs", c, s, way), own, ZR[c].at[i * 4 + s], device(x, y, zat(way), k))
        else:
            arrived(("zc", c, 0), ZC[c].at[z])
            total = combined(c, me) + ZC[c][z].astype(F32)
            for i, way in enumerate((1, -1)):
                arrived(("rs", c, 3, way), ZR[c].at[i * 4 + 3])
                total = total + ZR[c][i * 4 + 3].astype(F32)
            out_ref[:, lo:hi] = total.astype(BF16)

    gather_step(0, 1)
    make_meta()
    send_meta()
    for t in range(2, 5 + 2 * NC):
        for c in range(NC):
            s = t - 2 * c
            if 1 <= s <= 5 and (c, s) != (0, 1):
                gather_step(c, s)
        if t == 3:
            build_pick()
        for c in range(NC):
            if t - 2 * c == 5:
                x_stage(c)
                if c:
                    y_stage(c - 1)
        if t == 6:
            load_weights()
    y_stage(NC - 1)
    expert(0)
    drain()
    build_combine()
    for j in (1, 3, 2):
        expert(j)
        if j == 3:
            for c in range(NC):
                halves(c, 1)
    for c in range(NC):
        halves(c, 0)
    order = sorted((s + 2 * c, -c, c, s) for c in range(NC) for s in range(5))
    started = set()
    for _, _, c, s in order:
        if c not in started:
            started.add(c)
            combine_sibling(c)
        scatter_step(c, s)
    drain()

    def end_one(j, carry):
        meta_copy(j).wait_send()
        return carry
    lax.fori_loop(1, NSRC, end_one, 0)
    assert len(ids_of) <= send_sems.shape[0]


def moe(ids, weights, tokens, w_in, w_down):
    rows, model = tokens.shape
    widths = [hi - lo for lo, hi in CHUNKS]
    lead = (
        (NSRC, rows), (3, 2, UNIT), (5, NX, UNIT), (4, NX, UNIT), (3, NX, UNIT), (2, NX, UNIT), (NX, 2, UNIT),
        (NZ, rows), (8, rows))
    buffers = [pltpu.VMEM(shape + (width,), BF16) for shape in lead for width in widths]
    copies = NC * (8 + 8 + 3 + 3 + 3 + 6 + 8 + 8)
    vmem = pl.BlockSpec(memory_space=pltpu.VMEM)
    hbm = pl.BlockSpec(memory_space=pl.ANY)
    return pl.pallas_call(
        moe_kernel,
        out_shape=jax.ShapeDtypeStruct((rows, model), BF16),
        in_specs=[vmem, vmem, vmem, hbm, hbm],
        out_specs=vmem,
        scratch_shapes=buffers + [
            pltpu.VMEM((NSRC, 8, 128), F32),
            pltpu.VMEM((ROWS, NSRC * rows), BF16),
            pltpu.VMEM((NSRC * rows, ROWS), BF16),
            pltpu.VMEM(w_in.shape, BF16),
            pltpu.VMEM((w_in.shape[0], w_down.shape[0]), BF16),
            pltpu.VMEM(w_down.shape, BF16),
            pltpu.SemaphoreType.DMA((copies,)),
            pltpu.SemaphoreType.DMA((copies,)),
            pltpu.SemaphoreType.DMA((NSRC,)),
            pltpu.SemaphoreType.DMA((NSRC,)),
            pltpu.SemaphoreType.DMA((2,)),
        ],
        compiler_params=pltpu.CompilerParams(
            collective_id=0, has_side_effects=True, vmem_limit_bytes=60 * 1024 * 1024),
        cost_estimate=pl.CostEstimate(flops=16 * 10**9, bytes_accessed=7 * 10**6, transcendentals=10**6),
    )(ids, weights, tokens, w_in, w_down)


def local(tokens, expert_ids, route_weights, w_in, w_down, spare_source, spare_host):
    rep_count = lax.axis_size("rep")
    column_count = lax.axis_size("exp")
    group_count = rep_count // 2
    expert_count = group_count * column_count
    rep, column = lax.axis_index("rep"), lax.axis_index("exp")

    experts = jnp.arange(expert_count, dtype=jnp.int32)
    counts = jnp.sum((expert_ids.reshape(-1)[:, None] == experts[None, :]).astype(jnp.int32), axis=0)
    upper = jnp.where(rep >= group_count, counts, 0)
    both = lax.psum(jnp.stack([counts, upper]), ("rep", "exp"))

    mixed = moe(expert_ids, route_weights, tokens, w_in[0, 0], w_down[0, 0])

    residue = rep % group_count
    own = column * group_count + residue
    is_source = jnp.any(column == spare_source)
    load = jnp.take(both[0], own) - jnp.where(is_source, jnp.take(both[1], own), 0)
    copied = jnp.take(both[1], spare_source * group_count + residue)
    load = load + jnp.sum(jnp.where(column == spare_host, copied, 0))
    return mixed, load.astype(jnp.int32).reshape(1, 1)


def solution(mesh):
    placed = (
        P(("rep", "exp"), None),
        P(("rep", "exp"), None),
        P(("rep", "exp"), None),
        P("rep", "exp", None, None),
        P("rep", "exp", None, None),
        P(),
        P(),
    )
    return jax.shard_map(
        local,
        mesh=mesh,
        in_specs=placed,
        out_specs=(P(("rep", "exp"), None), P("rep", "exp")),
        check_vma=False,
    )
```

```python
import jax
import jax.numpy as jnp
from jax import lax
from jax.experimental import pallas as pl
from jax.experimental.pallas import tpu as pltpu
from jax.sharding import PartitionSpec as P

MESH = pl.DeviceIdType.MESH
F32 = jnp.float32
BF16 = jnp.bfloat16

NX, NY, NZ = 4, 4, 8
NSRC = 2 * NZ
CAP = 5
UNIT = NSRC * CAP
ROWS = NX * 2 * UNIT
CODE = 1024
CHUNKS = ((0, 512), (512, 1024), (1024, 1440))
NC = len(CHUNKS)
OFFS = (0, -1, 1, -2, 2, -3, 3, 4)


def device(x, y, z, k):
    return (y * 4 + lax.rem(z, 2) * 2 + k, x * 4 + lax.div(z, 2))


def moe_kernel(ids_ref, wts_ref, tok_ref, source_ref, host_ref, wi_hbm, wd_hbm, out_ref, load_ref, *scratch):
    T, G, XY, PP, RY, SS, RX, ZC, ZR = (scratch[i * NC:(i + 1) * NC] for i in range(9))
    meta, OH, CT, WI, WU, WD, CX, CY, CE, send_sems, recv_sems, meta_send, meta_recv, load_sems = scratch[9 * NC:]
    tok_rows = tok_ref.shape[0]
    half = tok_rows // 2
    ff = WD.shape[0]

    rep, ex = lax.axis_index("rep"), lax.axis_index("exp")
    y, k = lax.div(rep, 4), lax.rem(rep, 2)
    x = lax.div(ex, 4)
    z = lax.rem(ex, 4) * 2 + lax.rem(lax.div(rep, 2), 2)
    me = z * 2 + k
    p = lax.rem(y, 2)

    def zat(d):
        return lax.rem(z + d + NZ, NZ)

    def yat(d):
        return lax.rem(y + d + NY, NY)

    def xat(d):
        return lax.rem(x + d + NX, NX)

    ids_of = {}
    sends = []

    def sem_of(name):
        if name not in ids_of:
            ids_of[name] = len(ids_of)
        return ids_of[name]

    def send(name, src, dst, to):
        i = sem_of(name)
        copy = pltpu.make_async_remote_copy(
            src_ref=src, dst_ref=dst, send_sem=send_sems.at[i], recv_sem=recv_sems.at[i],
            device_id=to, device_id_type=MESH)
        copy.start()
        sends.append(copy)

    def arrived(name, dst):
        i = sem_of(name)
        pltpu.make_async_remote_copy(
            src_ref=dst, dst_ref=dst, send_sem=send_sems.at[i], recv_sem=recv_sems.at[i],
            device_id=device(x, y, z, 1 - k), device_id_type=MESH).wait_recv()

    def drain():
        for copy in sends:
            copy.wait_send()
        sends.clear()

    barrier = pltpu.get_barrier_semaphore()
    for j in range(1, NSRC):
        peer = lax.rem(me + j, NSRC)
        pl.semaphore_signal(barrier, inc=1, device_id=device(x, y, lax.div(peer, 2), lax.rem(peer, 2)), device_id_type=MESH)
    for j in range(1, NX):
        for i in range(NZ // 2):
            pl.semaphore_signal(barrier, inc=1, device_id=device(xat(j), y, zat(2 * i), k), device_id_type=MESH)
    for j in range(1, NY):
        pl.semaphore_signal(barrier, inc=1, device_id=device(x, yat(j), z, k), device_id_type=MESH)

    load_in = pltpu.make_async_copy(wi_hbm, WI, load_sems.at[0])
    load_down = pltpu.make_async_copy(wd_hbm, WD, load_sems.at[1])
    load_in.start()
    load_down.start()
    for c, (lo, hi) in enumerate(CHUNKS):
        T[c][me] = tok_ref[:, lo:hi]
    pl.semaphore_wait(barrier, NSRC - 1 + (NX - 1) * (NZ // 2) + NY - 1)

    def block(c, d, rows=None, core=None):
        ref = T[c].at[zat(d) * 2 + (k if core is None else core)]
        return ref if rows is None else ref.at[pl.ds(rows, half)]

    def to_sibling(c, d):
        send(("sib", c, d), block(c, d), block(c, d), device(x, y, z, 1 - k))

    def gather_step(c, s):
        if s == 1:
            to_send = ((1, block(c, 0)), (-1, block(c, 0)))
        else:
            for way in (1, -1):
                rows = None if s <= 4 else (0 if way == 1 else half)
                arrived(("ag", c, s - 1, way), block(c, -(s - 1) * way, rows))
            to_send = ()
            if s <= 4:
                to_send = tuple(
                    (way, block(c, -(s - 1) * way, None if s < 4 else (0 if way == 1 else half))) for way in (1, -1))
        for way, ref in to_send:
            send(("ag", c, s, way), ref, ref, device(x, y, zat(way), k))
        if s == 1:
            to_sibling(c, 0)
        elif s <= 4:
            to_sibling(c, -(s - 1))
            to_sibling(c, s - 1)
        else:
            to_sibling(c, 4)

    def make_meta():
        experts = lax.broadcasted_iota(jnp.int32, (tok_rows, 128), 1)
        total = jnp.zeros((tok_rows, 128), F32)
        hits = []
        for i in range(4):
            hit = (ids_ref[:, i:i + 1] == experts).astype(F32)
            hits.append(hit)
            total = total + hit
        before = (lax.broadcasted_iota(jnp.int32, (tok_rows, tok_rows), 0)
                  > lax.broadcasted_iota(jnp.int32, (tok_rows, tok_rows), 1)).astype(BF16)
        earlier = jnp.dot(before, total.astype(BF16), preferred_element_type=F32)
        table = jnp.zeros((tok_rows, 128), F32)
        for i in range(4):
            rank = jnp.sum(earlier * hits[i], axis=1, keepdims=True)
            e = ids_ref[:, i:i + 1]
            owner = ((e >> 3) & 3) * 4 + ((e >> 1) & 1) * 2 + (e & 1)
            place = ((e >> 5) * 2 + ((e >> 2) & 1)) * UNIT
            code = (owner * CODE + place).astype(F32) + rank
            table = jnp.where(experts == i, code, table)
            table = jnp.where(experts == 4 + i, wts_ref[:, i:i + 1], table)
        meta[me] = table.T[0:8, :]

    def send_meta():
        def one(j, carry):
            peer = lax.rem(me + j, NSRC)
            pltpu.make_async_remote_copy(
                src_ref=meta.at[me], dst_ref=meta.at[me], send_sem=meta_send.at[j], recv_sem=meta_recv.at[j],
                device_id=device(x, y, lax.div(peer, 2), lax.rem(peer, 2)), device_id_type=MESH).start()
            return carry
        lax.fori_loop(1, NSRC, one, 0)

    def meta_copy(j):
        peer = lax.rem(me + NSRC - j, NSRC)
        return pltpu.make_async_remote_copy(
            src_ref=meta.at[peer], dst_ref=meta.at[peer], send_sem=meta_send.at[j], recv_sem=meta_recv.at[j],
            device_id=device(x, y, lax.div(peer, 2), lax.rem(peer, 2)), device_id_type=MESH)

    def build_pick():
        def wait_one(j, carry):
            meta_copy(j).wait_recv()
            return carry
        lax.fori_loop(1, NSRC, wait_one, 0)

        def one(s, carry):
            row = lax.broadcasted_iota(jnp.int32, (ROWS, tok_rows), 0).astype(F32)
            shift = (s * CAP - me * CODE).astype(F32)
            codes = meta[s] + shift
            hit = row == codes[0:1, :]
            for i in range(1, 4):
                hit = jnp.logical_or(hit, row == codes[i:i + 1, :])
            OH[:, pl.ds(pl.multiple_of(s * tok_rows, tok_rows), tok_rows)] = jnp.where(hit, 1.0, 0.0).astype(BF16)
            return carry
        lax.fori_loop(0, NSRC, one, 0)

    def build_combine():
        def one(s, carry):
            col = lax.broadcasted_iota(jnp.int32, (tok_rows, ROWS), 1).astype(F32)
            shift = (s * CAP - me * CODE).astype(F32)
            info = meta[s].T
            total = jnp.zeros((tok_rows, ROWS), F32)
            for i in range(4):
                total = jnp.where(col == info[:, i:i + 1] + shift, info[:, 4 + i:5 + i], total)
            CT[pl.ds(pl.multiple_of(s * tok_rows, tok_rows), tok_rows), :] = total.astype(BF16)
            return carry
        lax.fori_loop(0, NSRC, one, 0)

    def count_pairs():
        codes = meta[...] - (me * CODE).astype(F32)
        valid = lax.broadcasted_iota(jnp.int32, codes.shape, 1) < 4
        unit = lax.broadcasted_iota(jnp.int32, (8, 128), 0)
        table = jnp.zeros((8, 128), F32)
        for u in range(2 * NX):
            inside = jnp.logical_and(valid, jnp.logical_and(codes >= u * UNIT, codes < (u + 1) * UNIT))
            hits = jnp.sum(jnp.sum(jnp.where(inside, 1.0, 0.0), axis=0), axis=0, keepdims=True)
            table = jnp.where(unit == u, hits, table)
        CX[x] = table
        for j in range(1, NX):
            send(("cx", j), CX.at[x], CX.at[x], device(xat(j), y, z, k))

    def count_along_y():
        for j in range(1, NX):
            arrived(("cx", j), CX.at[xat(-j)])
        CY[y] = CX[0] + CX[1] + CX[2] + CX[3]
        for j in range(1, NY):
            send(("cy", j), CY.at[y], CY.at[y], device(x, yat(j), z, k))

    def count_upper():
        for j in range(1, NY):
            arrived(("cy", j), CY.at[yat(-j)])
        mine = lax.broadcasted_iota(jnp.int32, (8, 128), 0) == x * 2 + p
        CE[NSRC] = jnp.where(mine, CY[0] + CY[1], 0.0)
        CE[ex] = jnp.where(mine, CY[2] + CY[3], 0.0)
        for i in range(NX):
            for j in range(NZ // 2):
                if i or j:
                    send(("ce", i, j), CE.at[ex], CE.at[ex], device(xat(i), y, zat(2 * j), k))

    def finish_load():
        for i in range(NX):
            for j in range(NZ // 2):
                if i or j:
                    column = xat(-i) * 4 + lax.div(zat(NZ - 2 * j), 2)
                    arrived(("ce", i, j), CE.at[column])
        total = CE[NSRC]
        upper = CE[ex]
        for h in range(source_ref.shape[0]):
            upper = jnp.where(source_ref[h] == ex, 0.0, upper)
        total = total + upper
        for h in range(source_ref.shape[0]):
            for i in range(NSRC):
                taken = jnp.logical_and(host_ref[h] == ex, source_ref[h] == i)
                total = total + jnp.where(taken, CE[i], 0.0)
        summed = jnp.sum(jnp.sum(total, axis=0, keepdims=True), axis=1, keepdims=True)
        load_ref[...] = summed.astype(jnp.int32)

    def x_stage(c):
        width = CHUNKS[c][1] - CHUNKS[c][0]
        for d in OFFS:
            arrived(("sib", c, d), block(c, d, core=1 - k))
        for j in (2, 1, 3, 0):
            xp = xat(j)
            picked = jnp.dot(
                OH[pl.ds(pl.multiple_of(xp * 2 * UNIT, 2 * UNIT), 2 * UNIT), :],
                T[c][...].reshape(NSRC * tok_rows, width),
                preferred_element_type=F32).astype(BF16).reshape(2, UNIT, width)
            if j == 0:
                XY[c][0, x] = picked[0]
                XY[c][1, x] = picked[1]
            else:
                G[c][j - 1] = picked
                send(("x", c, j), G[c].at[j - 1], XY[c].at[pl.ds(0, 2), x], device(xp, y, z, k))

    def y_stage(c):
        for j in (1, 3, 2):
            arrived(("x", c, j), XY[c].at[pl.ds(0, 2), xat(-j)])
        for j in (1, 3, 2):
            a = lax.rem(p + j, 2)
            send(("y", c, j), XY[c].at[a], XY[c].at[1 + j], device(x, yat(j), z, k))

    def load_weights():
        load_in.wait()
        load_down.wait()

        def one(i, carry):
            rows = pl.ds(pl.multiple_of(i * 160, 16), 160)
            WU[rows, :] = WI[rows, ff:2 * ff]
            return carry
        lax.fori_loop(0, WI.shape[0] // 160, one, 0)

    def expert(j):
        slot = p if j == 0 else 1 + j
        if j:
            for c in range(NC):
                arrived(("y", c, j), XY[c].at[slot])

        def one(q, carry):
            gate = up = None
            for c, (lo, hi) in enumerate(CHUNKS):
                rows = XY[c][slot, pl.ds(q * 2, 2)].reshape(2 * UNIT, hi - lo)
                g = jnp.dot(rows, WI[lo:hi, 0:ff], preferred_element_type=F32)
                u = jnp.dot(rows, WU[lo:hi, :], preferred_element_type=F32)
                gate, up = (g, u) if gate is None else (gate + g, up + u)
            hidden = ((up + 1.0) * gate * jax.nn.sigmoid(1.702 * gate)).astype(BF16)
            for c, (lo, hi) in enumerate(CHUNKS):
                part = jnp.dot(hidden, WD[:, lo:hi], preferred_element_type=F32).astype(BF16)
                PP[c][j, pl.ds(q * 2, 2)] = part.reshape(2, UNIT, hi - lo)
            return carry
        lax.fori_loop(0, 2, one, 0)
        if j:
            for c in range(NC):
                send(("ry", c, j), PP[c].at[j], RY[c].at[j - 1], device(x, yat(-j), z, k))

    def halves(c, odd):
        if odd:
            arrived(("ry", c, 1), RY[c].at[0])
            arrived(("ry", c, 3), RY[c].at[2])
            first, second = RY[c].at[0], RY[c].at[2]
        else:
            arrived(("ry", c, 2), RY[c].at[1])
            first, second = PP[c].at[0], RY[c].at[1]
        a = lax.rem(p + odd, 2)

        def one(i, carry):
            SS[c][odd, i] = (first[i].astype(F32) + second[i].astype(F32)).astype(BF16)
            return carry
        lax.fori_loop(0, NX, one, 0)
        for j in (2, 1, 3):
            xs = xat(j)
            send(("rx", c, odd, j), SS[c].at[odd, xs], RX[c].at[x, a], device(xs, y, z, k))
        RX[c][x, a] = SS[c][odd, x]

    def combined(c, s):
        width = CHUNKS[c][1] - CHUNKS[c][0]
        return jnp.dot(
            CT[pl.ds(pl.multiple_of(s * tok_rows, tok_rows), tok_rows), :],
            RX[c][...].reshape(ROWS, width), preferred_element_type=F32)

    def combine_sibling(c):
        for odd in (1, 0):
            a = lax.rem(p + odd, 2)
            for j in (2, 1, 3):
                arrived(("rx", c, odd, j), RX[c].at[xat(-j), a])
        for d in OFFS[::-1]:
            s = zat(d) * 2 + 1 - k
            T[c][s] = combined(c, s).astype(BF16)
            send(("zc", c, d), T[c].at[s], ZC[c].at[zat(d)], device(x, y, z, 1 - k))

    def scatter_step(c, s):
        lo, hi = CHUNKS[c]
        if s == 0:
            arrived(("zc", c, 4), ZC[c].at[zat(4)])
            own = T[c].at[zat(4) * 2 + k]
            own[...] = (combined(c, zat(4) * 2 + k) + ZC[c][zat(4)].astype(F32)).astype(BF16)
            for i, way in enumerate((1, -1)):
                rows = pl.ds(i * half, half)
                send(("rs", c, 0, way), own.at[rows], ZR[c].at[i * 4, rows], device(x, y, zat(way), k))
        elif s < 4:
            for i, way in enumerate((1, -1)):
                d = way * (4 - s)
                arrived(("zc", c, d), ZC[c].at[zat(d)])
                total = combined(c, zat(d) * 2 + k) + ZC[c][zat(d)].astype(F32)
                own = T[c].at[zat(d) * 2 + k]
                if s == 1:
                    rows = pl.ds(i * half, half)
                    arrived(("rs", c, 0, way), ZR[c].at[i * 4, rows])
                    mine = total[i * half:(i + 1) * half] + ZR[c][i * 4, rows].astype(F32)
                    own[rows, :] = mine.astype(BF16)
                    other = 1 - i
                    own[pl.ds(other * half, half), :] = total[other * half:(other + 1) * half].astype(BF16)
                else:
                    arrived(("rs", c, s - 1, way), ZR[c].at[i * 4 + s - 1])
                    own[...] = (total + ZR[c][i * 4 + s - 1].astype(F32)).astype(BF16)
                send(("rs", c, s, way), own, ZR[c].at[i * 4 + s], device(x, y, zat(way), k))
        else:
            arrived(("zc", c, 0), ZC[c].at[z])
            total = combined(c, me) + ZC[c][z].astype(F32)
            for i, way in enumerate((1, -1)):
                arrived(("rs", c, 3, way), ZR[c].at[i * 4 + 3])
                total = total + ZR[c][i * 4 + 3].astype(F32)
            out_ref[:, lo:hi] = total.astype(BF16)

    gather_step(0, 1)
    make_meta()
    send_meta()
    for t in range(2, 5 + 2 * NC):
        for c in range(NC):
            s = t - 2 * c
            if 1 <= s <= 5 and (c, s) != (0, 1):
                gather_step(c, s)
        if t == 3:
            build_pick()
            count_pairs()
        for c in range(NC):
            if t - 2 * c == 5:
                x_stage(c)
                if c:
                    y_stage(c - 1)
        if t == 6:
            load_weights()
            count_along_y()
    y_stage(NC - 1)
    count_upper()
    expert(0)
    drain()
    build_combine()
    for j in (1, 3, 2):
        expert(j)
        if j == 3:
            for c in range(NC):
                halves(c, 1)
    finish_load()
    for c in range(NC):
        halves(c, 0)
    order = sorted((s + 2 * c, -c, c, s) for c in range(NC) for s in range(5))
    started = set()
    for _, _, c, s in order:
        if c not in started:
            started.add(c)
            combine_sibling(c)
        scatter_step(c, s)
    drain()

    def end_one(j, carry):
        meta_copy(j).wait_send()
        return carry
    lax.fori_loop(1, NSRC, end_one, 0)
    assert len(ids_of) <= send_sems.shape[0]


def moe(ids, weights, tokens, source, host, w_in, w_down):
    rows, model = tokens.shape
    widths = [hi - lo for lo, hi in CHUNKS]
    lead = (
        (NSRC, rows), (3, 2, UNIT), (5, NX, UNIT), (4, NX, UNIT), (3, NX, UNIT), (2, NX, UNIT), (NX, 2, UNIT),
        (NZ, rows), (8, rows))
    buffers = [pltpu.VMEM(shape + (width,), BF16) for shape in lead for width in widths]
    copies = NC * (8 + 8 + 3 + 3 + 3 + 6 + 8 + 8) + 3 + 3 + 15
    vmem = pl.BlockSpec(memory_space=pltpu.VMEM)
    smem = pl.BlockSpec(memory_space=pltpu.SMEM)
    hbm = pl.BlockSpec(memory_space=pl.ANY)
    return pl.pallas_call(
        moe_kernel,
        out_shape=(jax.ShapeDtypeStruct((rows, model), BF16), jax.ShapeDtypeStruct((1, 1), jnp.int32)),
        in_specs=[vmem, vmem, vmem, smem, smem, hbm, hbm],
        out_specs=(vmem, vmem),
        scratch_shapes=buffers + [
            pltpu.VMEM((NSRC, 8, 128), F32),
            pltpu.VMEM((ROWS, NSRC * rows), BF16),
            pltpu.VMEM((NSRC * rows, ROWS), BF16),
            pltpu.VMEM(w_in.shape, BF16),
            pltpu.VMEM((w_in.shape[0], w_down.shape[0]), BF16),
            pltpu.VMEM(w_down.shape, BF16),
            pltpu.VMEM((NX, 8, 128), F32),
            pltpu.VMEM((NY, 8, 128), F32),
            pltpu.VMEM((NSRC + 1, 8, 128), F32),
            pltpu.SemaphoreType.DMA((copies,)),
            pltpu.SemaphoreType.DMA((copies,)),
            pltpu.SemaphoreType.DMA((NSRC,)),
            pltpu.SemaphoreType.DMA((NSRC,)),
            pltpu.SemaphoreType.DMA((2,)),
        ],
        compiler_params=pltpu.CompilerParams(
            collective_id=0, has_side_effects=True, vmem_limit_bytes=60 * 1024 * 1024),
        cost_estimate=pl.CostEstimate(flops=16 * 10**9, bytes_accessed=7 * 10**6, transcendentals=10**6),
    )(ids, weights, tokens, source, host, w_in, w_down)


def local(tokens, expert_ids, route_weights, w_in, w_down, spare_source, spare_host):
    return moe(expert_ids, route_weights, tokens, spare_source, spare_host, w_in[0, 0], w_down[0, 0])


def solution(mesh):
    placed = (
        P(("rep", "exp"), None),
        P(("rep", "exp"), None),
        P(("rep", "exp"), None),
        P("rep", "exp", None, None),
        P("rep", "exp", None, None),
        P(),
        P(),
    )
    return jax.shard_map(
        local,
        mesh=mesh,
        in_specs=placed,
        out_specs=(P(("rep", "exp"), None), P("rep", "exp")),
        check_vma=False,
    )
```

```python
import jax
import jax.numpy as jnp
from jax import lax
from jax.experimental import pallas as pl
from jax.experimental.pallas import tpu as pltpu
from jax.sharding import PartitionSpec as P

MESH = pl.DeviceIdType.MESH
F32 = jnp.float32
BF16 = jnp.bfloat16

NX, NY, NZ = 4, 4, 8
NSRC = 2 * NZ
CAP = 5
UNIT = NSRC * CAP
ROWS = NX * 2 * UNIT
CODE = 1024
CHUNKS = ((0, 256), (256, 768), (768, 1280), (1280, 1440))
BEGIN = (0, 1, 3, 5)
NC = len(CHUNKS)
OFFS = (0, -1, 1, -2, 2, -3, 3, 4)


def device(x, y, z, k):
    return (y * 4 + lax.rem(z, 2) * 2 + k, x * 4 + lax.div(z, 2))


def moe_kernel(ids_ref, wts_ref, tok_ref, source_ref, host_ref, wi_hbm, wd_hbm, out_ref, load_ref, *scratch):
    T, G, XY, PP, RY, SS, RX, ZC, ZR, OWN = (scratch[i * NC:(i + 1) * NC] for i in range(10))
    meta, OH, CT, WI, WU, WD, HID, CX, CY, CE, send_sems, recv_sems, meta_send, meta_recv, load_sems = scratch[10 * NC:]
    tok_rows = tok_ref.shape[1]
    half = tok_rows // 2
    ff = WD.shape[0]

    rep, ex = lax.axis_index("rep"), lax.axis_index("exp")
    y, k = lax.div(rep, 4), lax.rem(rep, 2)
    x = lax.div(ex, 4)
    z = lax.rem(ex, 4) * 2 + lax.rem(lax.div(rep, 2), 2)
    me = k * NZ + z
    p = lax.rem(y, 2)

    def zat(d):
        return lax.rem(z + d + NZ, NZ)

    def yat(d):
        return lax.rem(y + d + NY, NY)

    def xat(d):
        return lax.rem(x + d + NX, NX)

    ids_of = {}
    sends = []

    def sem_of(name):
        if name not in ids_of:
            ids_of[name] = len(ids_of)
        return ids_of[name]

    def send(name, src, dst, to):
        i = sem_of(name)
        copy = pltpu.make_async_remote_copy(
            src_ref=src, dst_ref=dst, send_sem=send_sems.at[i], recv_sem=recv_sems.at[i],
            device_id=to, device_id_type=MESH)
        copy.start()
        sends.append(copy)

    def arrived(name, dst):
        i = sem_of(name)
        pltpu.make_async_remote_copy(
            src_ref=dst, dst_ref=dst, send_sem=send_sems.at[i], recv_sem=recv_sems.at[i],
            device_id=device(x, y, z, 1 - k), device_id_type=MESH).wait_recv()

    def drain():
        for copy in sends:
            copy.wait_send()
        sends.clear()

    barrier = pltpu.get_barrier_semaphore()
    for j in range(1, NSRC):
        peer = lax.rem(me + j, NSRC)
        pl.semaphore_signal(barrier, inc=1, device_id=device(x, y, lax.rem(peer, NZ), lax.div(peer, NZ)), device_id_type=MESH)
    for j in range(1, NX):
        pl.semaphore_signal(barrier, inc=1, device_id=device(xat(j), y, z, k), device_id_type=MESH)
    for j in range(1, NY):
        pl.semaphore_signal(barrier, inc=1, device_id=device(x, yat(j), z, k), device_id_type=MESH)

    load_in = pltpu.make_async_copy(wi_hbm, WI, load_sems.at[0])
    load_down = pltpu.make_async_copy(wd_hbm, WD, load_sems.at[1])
    load_in.start()
    load_down.start()
    for c, (lo, hi) in enumerate(CHUNKS):
        T[c][me] = tok_ref[lo:hi, :].T
    pl.semaphore_wait(barrier, NSRC - 1 + NX - 1 + NY - 1)

    def block(c, d, rows=None, core=None):
        ref = T[c].at[(k if core is None else core) * NZ + zat(d)]
        return ref if rows is None else ref.at[pl.ds(rows, half)]

    def to_sibling(c, d):
        send(("sib", c, d), block(c, d), block(c, d), device(x, y, z, 1 - k))

    def gather_step(c, s):
        if s == 1:
            to_send = ((1, block(c, 0)), (-1, block(c, 0)))
        else:
            for way in (1, -1):
                rows = None if s <= 4 else (0 if way == 1 else half)
                arrived(("ag", c, s - 1, way), block(c, -(s - 1) * way, rows))
            to_send = ()
            if s <= 4:
                to_send = tuple(
                    (way, block(c, -(s - 1) * way, None if s < 4 else (0 if way == 1 else half))) for way in (1, -1))
        for way, ref in to_send:
            send(("ag", c, s, way), ref, ref, device(x, y, zat(way), k))
        if s == 1:
            to_sibling(c, 0)
        elif s <= 4:
            to_sibling(c, -(s - 1))
            to_sibling(c, s - 1)
        else:
            to_sibling(c, 4)

    def make_meta():
        experts = lax.broadcasted_iota(jnp.int32, (128, tok_rows), 0)
        hits = [(ids_ref[i:i + 1, :] == experts).astype(F32) for i in range(4)]
        total = hits[0] + hits[1] + hits[2] + hits[3]
        before = (lax.broadcasted_iota(jnp.int32, (tok_rows, tok_rows), 0)
                  < lax.broadcasted_iota(jnp.int32, (tok_rows, tok_rows), 1)).astype(F32).astype(BF16)
        earlier = jnp.dot(total.astype(BF16), before, preferred_element_type=F32)
        for i in range(4):
            rank = jnp.sum(earlier * hits[i], axis=0, keepdims=True)
            e = ids_ref[i:i + 1, :]
            owner = (e & 1) * NZ + ((e >> 3) & 3) * 2 + ((e >> 1) & 1)
            place = ((e >> 5) * 2 + ((e >> 2) & 1)) * UNIT
            meta[me, i:i + 1, :] = (owner * CODE + place).astype(F32) + rank
            meta[me, 4 + i:5 + i, :] = wts_ref[i:i + 1, :]

    def send_meta():
        def one(j, carry):
            peer = lax.rem(me + j, NSRC)
            pltpu.make_async_remote_copy(
                src_ref=meta.at[me], dst_ref=meta.at[me], send_sem=meta_send.at[j], recv_sem=meta_recv.at[j],
                device_id=device(x, y, lax.rem(peer, NZ), lax.div(peer, NZ)), device_id_type=MESH).start()
            return carry
        lax.fori_loop(1, NSRC, one, 0)

    def meta_copy(j):
        peer = lax.rem(me + NSRC - j, NSRC)
        return pltpu.make_async_remote_copy(
            src_ref=meta.at[peer], dst_ref=meta.at[peer], send_sem=meta_send.at[j], recv_sem=meta_recv.at[j],
            device_id=device(x, y, lax.rem(peer, NZ), lax.div(peer, NZ)), device_id_type=MESH)

    def build_pick():
        def wait_one(j, carry):
            meta_copy(j).wait_recv()
            return carry
        lax.fori_loop(1, NSRC, wait_one, 0)

        def one(s, carry):
            row = lax.broadcasted_iota(jnp.int32, (ROWS, tok_rows), 0).astype(F32)
            shift = (s * CAP - me * CODE).astype(F32)
            codes = meta[s] + shift
            hit = row == codes[0:1, :]
            for i in range(1, 4):
                hit = jnp.logical_or(hit, row == codes[i:i + 1, :])
            OH[:, pl.ds(pl.multiple_of(s * tok_rows, tok_rows), tok_rows)] = jnp.where(hit, 1.0, 0.0).astype(BF16)
            return carry
        lax.fori_loop(0, NSRC, one, 0)

    def build_combine():
        def one(s, carry):
            col = lax.broadcasted_iota(jnp.int32, (tok_rows, ROWS), 1).astype(F32)
            shift = (s * CAP - me * CODE).astype(F32)
            info = meta[s].T
            total = jnp.zeros((tok_rows, ROWS), F32)
            for i in range(4):
                total = jnp.where(col == info[:, i:i + 1] + shift, info[:, 4 + i:5 + i], total)
            CT[pl.ds(pl.multiple_of(s * tok_rows, tok_rows), tok_rows), :] = total.astype(BF16)
            return carry
        lax.fori_loop(0, NSRC, one, 0)

    def count_pairs():
        codes = meta[...] - (me * CODE).astype(F32)
        valid = lax.broadcasted_iota(jnp.int32, codes.shape, 1) < 4
        unit = lax.broadcasted_iota(jnp.int32, (8, 128), 0)
        table = jnp.zeros((8, 128), F32)
        for u in range(2 * NX):
            inside = jnp.logical_and(valid, jnp.logical_and(codes >= u * UNIT, codes < (u + 1) * UNIT))
            hits = jnp.sum(jnp.sum(jnp.where(inside, 1.0, 0.0), axis=0), axis=0, keepdims=True)
            table = jnp.where(unit == u, hits, table)
        CX[x] = table
        for j in range(1, NX):
            send(("cx", j), CX.at[x], CX.at[x], device(xat(j), y, z, k))

    def count_along_y():
        for j in range(1, NX):
            arrived(("cx", j), CX.at[xat(-j)])
        CY[y] = CX[0] + CX[1] + CX[2] + CX[3]
        for j in range(1, NY):
            send(("cy", j), CY.at[y], CY.at[y], device(x, yat(j), z, k))

    def count_upper():
        for j in range(1, NY):
            arrived(("cy", j), CY.at[yat(-j)])
        mine = lax.broadcasted_iota(jnp.int32, (8, 128), 0) == x * 2 + p
        CE[NSRC] = jnp.where(mine, CY[0] + CY[1], 0.0)
        CE[ex] = jnp.where(mine, CY[2] + CY[3], 0.0)
        for j in range(1, NX):
            send(("ce", j), CE.at[ex], CE.at[ex], device(xat(j), y, z, k))

    def column(i, j):
        return i * 4 + lax.div(zat(NZ - 2 * j), 2)

    def spread_upper():
        for j in range(1, NX):
            arrived(("ce", j), CE.at[xat(-j) * 4 + lax.div(z, 2)])
        for j in range(1, NZ // 2):
            for i in range(NX):
                send(("cz", i, j), CE.at[column(i, 0)], CE.at[column(i, 0)], device(x, y, zat(2 * j), k))

    def finish_load():
        for j in range(1, NZ // 2):
            for i in range(NX):
                arrived(("cz", i, j), CE.at[column(i, j)])
        total = CE[NSRC]
        upper = CE[ex]
        for h in range(source_ref.shape[0]):
            upper = jnp.where(source_ref[h] == ex, 0.0, upper)
        total = total + upper
        for h in range(source_ref.shape[0]):
            for i in range(NSRC):
                taken = jnp.logical_and(host_ref[h] == ex, source_ref[h] == i)
                total = total + jnp.where(taken, CE[i], 0.0)
        summed = jnp.sum(jnp.sum(total, axis=0, keepdims=True), axis=1, keepdims=True)
        load_ref[...] = summed.astype(jnp.int32)

    def x_stage(c):
        width = CHUNKS[c][1] - CHUNKS[c][0]
        for d in OFFS:
            arrived(("sib", c, d), block(c, d, core=1 - k))
        picked = jnp.dot(OH[...], T[c][...].reshape(NSRC * tok_rows, width), preferred_element_type=F32)
        G[c][...] = picked.astype(BF16).reshape(NX, 2, UNIT, width)
        for j in (2, 1, 3):
            xp = xat(j)
            send(("x", c, j), G[c].at[xp], XY[c].at[pl.ds(0, 2), x], device(xp, y, z, k))
        XY[c][0, x] = G[c][x, 0]
        XY[c][1, x] = G[c][x, 1]

    def y_stage(c):
        for j in (1, 3, 2):
            arrived(("x", c, j), XY[c].at[pl.ds(0, 2), xat(-j)])
        for j in (1, 3, 2):
            a = lax.rem(p + j, 2)
            send(("y", c, j), XY[c].at[a], XY[c].at[1 + j], device(x, yat(j), z, k))

    def load_weights():
        load_in.wait()
        load_down.wait()

        def one(i, carry):
            rows = pl.ds(pl.multiple_of(i * 160, 16), 160)
            WU[rows, :] = WI[rows, ff:2 * ff]
            return carry
        lax.fori_loop(0, WI.shape[0] // 160, one, 0)

    def expert(j):
        slot = p if j == 0 else 1 + j
        gate = up = None
        for c, (lo, hi) in enumerate(CHUNKS):
            if j:
                arrived(("y", c, j), XY[c].at[slot])
            rows = XY[c][slot].reshape(NX * UNIT, hi - lo)
            g = jnp.dot(rows, WI[lo:hi, 0:ff], preferred_element_type=F32)
            u = jnp.dot(rows, WU[lo:hi, :], preferred_element_type=F32)
            gate, up = (g, u) if gate is None else (gate + g, up + u)
        HID[j * NX * UNIT:(j + 1) * NX * UNIT, :] = ((up + 1.0) * gate * jax.nn.sigmoid(1.702 * gate)).astype(BF16)

    def down(c):
        lo, hi = CHUNKS[c]
        part = jnp.dot(HID[...], WD[:, lo:hi], preferred_element_type=F32).astype(BF16)
        PP[c][...] = part.reshape(NY, NX, UNIT, hi - lo)
        for j in (1, 3, 2):
            send(("ry", c, j), PP[c].at[j], RY[c].at[j - 1], device(x, yat(-j), z, k))

    def halves(c):
        for j in (1, 3, 2):
            arrived(("ry", c, j), RY[c].at[j - 1])

        def one(i, carry):
            SS[c][p, i] = (PP[c][0, i].astype(F32) + RY[c][1, i].astype(F32)).astype(BF16)
            SS[c][1 - p, i] = (RY[c][0, i].astype(F32) + RY[c][2, i].astype(F32)).astype(BF16)
            return carry
        lax.fori_loop(0, NX, one, 0)
        for j in (2, 1, 3):
            xs = xat(j)
            send(("rx", c, j), SS[c].at[pl.ds(0, 2), xs], RX[c].at[x], device(xs, y, z, k))
        RX[c][x, 0] = SS[c][0, x]
        RX[c][x, 1] = SS[c][1, x]

    def combine(c):
        lo, hi = CHUNKS[c]
        for j in (2, 1, 3):
            arrived(("rx", c, j), RX[c].at[xat(-j)])

        def all_rows(core):
            rows = CT[pl.ds(pl.multiple_of(core * NZ * tok_rows, tok_rows), NZ * tok_rows), :]
            total = jnp.dot(rows, RX[c][...].reshape(ROWS, hi - lo), preferred_element_type=F32)
            return total.reshape(NZ, tok_rows, hi - lo)
        other = pl.ds((1 - k) * NZ, NZ)
        T[c][other] = all_rows(1 - k).astype(BF16)
        send(("zc", c), T[c].at[other], ZC[c], device(x, y, z, 1 - k))
        OWN[c][...] = all_rows(k)

    def scatter_step(c, s):
        lo, hi = CHUNKS[c]
        if s == 0:
            arrived(("zc", c), ZC[c])

        def partial(d, rows=slice(None)):
            return OWN[c][zat(d), rows] + ZC[c][zat(d), rows].astype(F32)

        if s == 0:
            own = T[c].at[k * NZ + zat(4)]
            own[...] = partial(4).astype(BF16)
            for i, way in enumerate((1, -1)):
                rows = pl.ds(i * half, half)
                send(("rs", c, 0, way), own.at[rows], ZR[c].at[i * 4, rows], device(x, y, zat(way), k))
        elif s < 4:
            for i, way in enumerate((1, -1)):
                d = way * (4 - s)
                own = T[c].at[k * NZ + zat(d)]
                if s == 1:
                    rows = pl.ds(i * half, half)
                    rest = pl.ds((1 - i) * half, half)
                    own[rest, :] = partial(d, rest).astype(BF16)
                    arrived(("rs", c, 0, way), ZR[c].at[i * 4, rows])
                    own[rows, :] = (partial(d, rows) + ZR[c][i * 4, rows].astype(F32)).astype(BF16)
                else:
                    arrived(("rs", c, s - 1, way), ZR[c].at[i * 4 + s - 1])
                    own[...] = (partial(d) + ZR[c][i * 4 + s - 1].astype(F32)).astype(BF16)
                send(("rs", c, s, way), own, ZR[c].at[i * 4 + s], device(x, y, zat(way), k))
        else:
            total = partial(0)
            for i, way in enumerate((1, -1)):
                arrived(("rs", c, 3, way), ZR[c].at[i * 4 + 3])
                total = total + ZR[c][i * 4 + 3].astype(F32)
            out_ref[lo:hi, :] = total.T.astype(BF16)

    gather_step(0, 1)
    make_meta()
    send_meta()
    waiting = []
    for t in range(2, 6 + BEGIN[-1]):
        for c in range(NC):
            s = t - BEGIN[c]
            if 1 <= s <= 5:
                gather_step(c, s)
        if t == 3:
            build_pick()
        while waiting:
            y_stage(waiting.pop())
        for c in range(NC):
            if t - BEGIN[c] == 5:
                x_stage(c)
                waiting.append(c)
                if c == 0:
                    count_pairs()
                    load_weights()
                if c == 2:
                    count_along_y()
    y_stage(NC - 1)
    count_upper()
    expert(0)
    build_combine()
    drain()
    spread_upper()
    for j in (1, 3, 2):
        expert(j)
    down(0)
    down(1)
    halves(0)
    down(2)
    combine(0)
    scatter_step(0, 0)
    halves(1)
    down(3)
    finish_load()
    scatter_step(0, 1)
    combine(1)
    scatter_step(1, 0)
    scatter_step(0, 2)
    halves(2)
    scatter_step(1, 1)
    scatter_step(0, 3)
    combine(2)
    scatter_step(2, 0)
    scatter_step(1, 2)
    scatter_step(0, 4)
    halves(3)
    scatter_step(2, 1)
    scatter_step(1, 3)
    combine(3)
    scatter_step(3, 0)
    scatter_step(2, 2)
    scatter_step(3, 1)
    scatter_step(1, 4)
    scatter_step(2, 3)
    scatter_step(3, 2)
    scatter_step(2, 4)
    scatter_step(3, 3)
    scatter_step(3, 4)
    drain()

    def end_one(j, carry):
        meta_copy(j).wait_send()
        return carry
    lax.fori_loop(1, NSRC, end_one, 0)
    assert len(ids_of) <= send_sems.shape[0]


def moe(ids, weights, tokens, source, host, w_in, w_down):
    model, rows = tokens.shape
    widths = [hi - lo for lo, hi in CHUNKS]
    lead = (
        (NSRC, rows), (NX, 2, UNIT), (5, NX, UNIT), (4, NX, UNIT), (3, NX, UNIT), (2, NX, UNIT), (NX, 2, UNIT),
        (NZ, rows), (8, rows))
    buffers = [pltpu.VMEM(shape + (width,), BF16) for shape in lead for width in widths]
    buffers += [pltpu.VMEM((NZ, rows, width), F32) for width in widths]
    copies = NC * (8 + 8 + 3 + 3 + 3 + 3 + 1 + 8) + 3 + 3 + 3 + 12
    vmem = pl.BlockSpec(memory_space=pltpu.VMEM)
    smem = pl.BlockSpec(memory_space=pltpu.SMEM)
    hbm = pl.BlockSpec(memory_space=pl.ANY)
    return pl.pallas_call(
        moe_kernel,
        out_shape=(jax.ShapeDtypeStruct((model, rows), BF16), jax.ShapeDtypeStruct((1, 1), jnp.int32)),
        in_specs=[vmem, vmem, vmem, smem, smem, hbm, hbm],
        out_specs=(vmem, vmem),
        scratch_shapes=buffers + [
            pltpu.VMEM((NSRC, 8, 128), F32),
            pltpu.VMEM((ROWS, NSRC * rows), BF16),
            pltpu.VMEM((NSRC * rows, ROWS), BF16),
            pltpu.VMEM(w_in.shape, BF16),
            pltpu.VMEM((w_in.shape[0], w_down.shape[0]), BF16),
            pltpu.VMEM(w_down.shape, BF16),
            pltpu.VMEM((NY * NX * UNIT, w_down.shape[0]), BF16),
            pltpu.VMEM((NX, 8, 128), F32),
            pltpu.VMEM((NY, 8, 128), F32),
            pltpu.VMEM((NSRC + 1, 8, 128), F32),
            pltpu.SemaphoreType.DMA((copies,)),
            pltpu.SemaphoreType.DMA((copies,)),
            pltpu.SemaphoreType.DMA((NSRC,)),
            pltpu.SemaphoreType.DMA((NSRC,)),
            pltpu.SemaphoreType.DMA((2,)),
        ],
        compiler_params=pltpu.CompilerParams(
            collective_id=0, has_side_effects=True, vmem_limit_bytes=60 * 1024 * 1024),
        cost_estimate=pl.CostEstimate(flops=16 * 10**9, bytes_accessed=7 * 10**6, transcendentals=10**6),
    )(ids, weights, tokens, source, host, w_in, w_down)


def local(tokens, expert_ids, route_weights, w_in, w_down, spare_source, spare_host):
    mixed, slot_load = moe(expert_ids.T, route_weights.T, tokens.T, spare_source, spare_host, w_in[0, 0], w_down[0, 0])
    return mixed.T, slot_load


def solution(mesh):
    placed = (
        P(("rep", "exp"), None),
        P(("rep", "exp"), None),
        P(("rep", "exp"), None),
        P("rep", "exp", None, None),
        P("rep", "exp", None, None),
        P(),
        P(),
    )
    return jax.shard_map(
        local,
        mesh=mesh,
        in_specs=placed,
        out_specs=(P(("rep", "exp"), None), P("rep", "exp")),
        check_vma=False,
    )
```

```python
import jax
import jax.numpy as jnp
from jax import lax
from jax.experimental import pallas as pl
from jax.experimental.pallas import tpu as pltpu
from jax.sharding import PartitionSpec as P

MESH = pl.DeviceIdType.MESH
F32 = jnp.float32
BF16 = jnp.bfloat16

NX, NY, NZ = 4, 4, 8
NSRC = 2 * NZ
CAP = 5
UNIT = NSRC * CAP
ROWS = NX * 2 * UNIT
CODE = 1024
CHUNKS = ((0, 256), (256, 768), (768, 1280), (1280, 1440))
BEGIN = (0, 2, 3, 1)
OUTWARD = (0, 3, 1, 2)
BACK = (0, 1, 2, 3)
NC = len(CHUNKS)
OFFS = (0, -1, 1, -2, 2, -3, 3, 4)


def device(x, y, z, k):
    return (y * 4 + lax.rem(z, 2) * 2 + k, x * 4 + lax.div(z, 2))


def moe_kernel(ids_ref, wts_ref, tok_ref, source_ref, host_ref, wi_hbm, wd_hbm, out_ref, load_ref, *scratch):
    T, G, XY, PP, RY, SS, RX, ZC, ZR, OWN = (scratch[i * NC:(i + 1) * NC] for i in range(10))
    meta, OH, CT, WI, WU, WD, HID, CX, CY, CE, send_sems, recv_sems, meta_send, meta_recv, load_sems = scratch[10 * NC:]
    tok_rows = tok_ref.shape[1]
    half = tok_rows // 2
    ff = WD.shape[0]

    rep, ex = lax.axis_index("rep"), lax.axis_index("exp")
    y, k = lax.div(rep, 4), lax.rem(rep, 2)
    x = lax.div(ex, 4)
    z = lax.rem(ex, 4) * 2 + lax.rem(lax.div(rep, 2), 2)
    me = k * NZ + z
    p = lax.rem(y, 2)

    def zat(d):
        return lax.rem(z + d + NZ, NZ)

    def yat(d):
        return lax.rem(y + d + NY, NY)

    def xat(d):
        return lax.rem(x + d + NX, NX)

    ids_of = {}
    sends = []

    def sem_of(name):
        if name not in ids_of:
            ids_of[name] = len(ids_of)
        return ids_of[name]

    def send(name, src, dst, to):
        i = sem_of(name)
        copy = pltpu.make_async_remote_copy(
            src_ref=src, dst_ref=dst, send_sem=send_sems.at[i], recv_sem=recv_sems.at[i],
            device_id=to, device_id_type=MESH)
        copy.start()
        sends.append(copy)

    def arrived(name, dst):
        i = sem_of(name)
        pltpu.make_async_remote_copy(
            src_ref=dst, dst_ref=dst, send_sem=send_sems.at[i], recv_sem=recv_sems.at[i],
            device_id=device(x, y, z, 1 - k), device_id_type=MESH).wait_recv()

    def drain():
        for copy in sends:
            copy.wait_send()
        sends.clear()

    barrier = pltpu.get_barrier_semaphore()
    for j in range(1, NSRC):
        peer = lax.rem(me + j, NSRC)
        pl.semaphore_signal(barrier, inc=1, device_id=device(x, y, lax.rem(peer, NZ), lax.div(peer, NZ)), device_id_type=MESH)
    for j in range(1, NX):
        pl.semaphore_signal(barrier, inc=1, device_id=device(xat(j), y, z, k), device_id_type=MESH)
    for j in range(1, NY):
        pl.semaphore_signal(barrier, inc=1, device_id=device(x, yat(j), z, k), device_id_type=MESH)

    load_in = pltpu.make_async_copy(wi_hbm, WI, load_sems.at[0])
    load_down = pltpu.make_async_copy(wd_hbm, WD, load_sems.at[1])
    load_in.start()
    load_down.start()
    for c, (lo, hi) in enumerate(CHUNKS):
        T[c][me] = tok_ref[lo:hi, :].T
    pl.semaphore_wait(barrier, NSRC - 1 + NX - 1 + NY - 1)

    def block(c, d, rows=None, core=None):
        ref = T[c].at[(k if core is None else core) * NZ + zat(d)]
        return ref if rows is None else ref.at[pl.ds(rows, half)]

    def to_sibling(c, d):
        send(("sib", c, d), block(c, d), block(c, d), device(x, y, z, 1 - k))

    def gather_step(c, s):
        if s == 1:
            to_send = ((1, block(c, 0)), (-1, block(c, 0)))
        else:
            for way in (1, -1):
                rows = None if s <= 4 else (0 if way == 1 else half)
                arrived(("ag", c, s - 1, way), block(c, -(s - 1) * way, rows))
            to_send = ()
            if s <= 4:
                to_send = tuple(
                    (way, block(c, -(s - 1) * way, None if s < 4 else (0 if way == 1 else half))) for way in (1, -1))
        for way, ref in to_send:
            send(("ag", c, s, way), ref, ref, device(x, y, zat(way), k))
        if s == 1:
            to_sibling(c, 0)
        elif s <= 4:
            to_sibling(c, -(s - 1))
            to_sibling(c, s - 1)
        else:
            to_sibling(c, 4)

    def make_meta():
        experts = lax.broadcasted_iota(jnp.int32, (128, tok_rows), 0)
        hits = [(ids_ref[i:i + 1, :] == experts).astype(F32) for i in range(4)]
        total = hits[0] + hits[1] + hits[2] + hits[3]
        before = (lax.broadcasted_iota(jnp.int32, (tok_rows, tok_rows), 0)
                  < lax.broadcasted_iota(jnp.int32, (tok_rows, tok_rows), 1)).astype(F32).astype(BF16)
        earlier = jnp.dot(total.astype(BF16), before, preferred_element_type=F32)
        for i in range(4):
            rank = jnp.sum(earlier * hits[i], axis=0, keepdims=True)
            e = ids_ref[i:i + 1, :]
            owner = (e & 1) * NZ + ((e >> 3) & 3) * 2 + ((e >> 1) & 1)
            place = ((e >> 5) * 2 + ((e >> 2) & 1)) * UNIT
            meta[me, i:i + 1, :] = (owner * CODE + place).astype(F32) + rank
            meta[me, 4 + i:5 + i, :] = wts_ref[i:i + 1, :]

    def send_meta():
        def one(j, carry):
            peer = lax.rem(me + j, NSRC)
            pltpu.make_async_remote_copy(
                src_ref=meta.at[me], dst_ref=meta.at[me], send_sem=meta_send.at[j], recv_sem=meta_recv.at[j],
                device_id=device(x, y, lax.rem(peer, NZ), lax.div(peer, NZ)), device_id_type=MESH).start()
            return carry
        lax.fori_loop(1, NSRC, one, 0)

    def meta_copy(j):
        peer = lax.rem(me + NSRC - j, NSRC)
        return pltpu.make_async_remote_copy(
            src_ref=meta.at[peer], dst_ref=meta.at[peer], send_sem=meta_send.at[j], recv_sem=meta_recv.at[j],
            device_id=device(x, y, lax.rem(peer, NZ), lax.div(peer, NZ)), device_id_type=MESH)

    def build_pick():
        def wait_one(j, carry):
            meta_copy(j).wait_recv()
            return carry
        lax.fori_loop(1, NSRC, wait_one, 0)

        def one(s, carry):
            row = lax.broadcasted_iota(jnp.int32, (ROWS, tok_rows), 0).astype(F32)
            shift = (s * CAP - me * CODE).astype(F32)
            codes = meta[s] + shift
            hit = row == codes[0:1, :]
            for i in range(1, 4):
                hit = jnp.logical_or(hit, row == codes[i:i + 1, :])
            OH[:, pl.ds(pl.multiple_of(s * tok_rows, tok_rows), tok_rows)] = jnp.where(hit, 1.0, 0.0).astype(BF16)
            return carry
        lax.fori_loop(0, NSRC, one, 0)

    def build_combine():
        def one(s, carry):
            col = lax.broadcasted_iota(jnp.int32, (tok_rows, ROWS), 1).astype(F32)
            shift = (s * CAP - me * CODE).astype(F32)
            info = meta[s].T
            total = jnp.zeros((tok_rows, ROWS), F32)
            for i in range(4):
                total = jnp.where(col == info[:, i:i + 1] + shift, info[:, 4 + i:5 + i], total)
            CT[pl.ds(pl.multiple_of(s * tok_rows, tok_rows), tok_rows), :] = total.astype(BF16)
            return carry
        lax.fori_loop(0, NSRC, one, 0)

    def count_pairs():
        codes = meta[...] - (me * CODE).astype(F32)
        valid = lax.broadcasted_iota(jnp.int32, codes.shape, 1) < 4
        unit = lax.broadcasted_iota(jnp.int32, (8, 128), 0)
        table = jnp.zeros((8, 128), F32)
        for u in range(2 * NX):
            inside = jnp.logical_and(valid, jnp.logical_and(codes >= u * UNIT, codes < (u + 1) * UNIT))
            hits = jnp.sum(jnp.sum(jnp.where(inside, 1.0, 0.0), axis=0), axis=0, keepdims=True)
            table = jnp.where(unit == u, hits, table)
        CX[x] = table
        for j in range(1, NX):
            send(("cx", j), CX.at[x], CX.at[x], device(xat(j), y, z, k))

    def count_along_y():
        for j in range(1, NX):
            arrived(("cx", j), CX.at[xat(-j)])
        CY[y] = CX[0] + CX[1] + CX[2] + CX[3]
        for j in range(1, NY):
            send(("cy", j), CY.at[y], CY.at[y], device(x, yat(j), z, k))

    def count_upper():
        for j in range(1, NY):
            arrived(("cy", j), CY.at[yat(-j)])
        mine = lax.broadcasted_iota(jnp.int32, (8, 128), 0) == x * 2 + p
        CE[NSRC] = jnp.where(mine, CY[0] + CY[1], 0.0)
        CE[ex] = jnp.where(mine, CY[2] + CY[3], 0.0)
        for j in range(1, NX):
            send(("ce", j), CE.at[ex], CE.at[ex], device(xat(j), y, z, k))

    def column(i, j):
        return i * 4 + lax.div(zat(NZ - 2 * j), 2)

    def spread_upper():
        for j in range(1, NX):
            arrived(("ce", j), CE.at[xat(-j) * 4 + lax.div(z, 2)])
        for j in range(1, NZ // 2):
            for i in range(NX):
                send(("cz", i, j), CE.at[column(i, 0)], CE.at[column(i, 0)], device(x, y, zat(2 * j), k))

    def finish_load():
        for j in range(1, NZ // 2):
            for i in range(NX):
                arrived(("cz", i, j), CE.at[column(i, j)])
        total = CE[NSRC]
        upper = CE[ex]
        for h in range(source_ref.shape[0]):
            upper = jnp.where(source_ref[h] == ex, 0.0, upper)
        total = total + upper
        for h in range(source_ref.shape[0]):
            for i in range(NSRC):
                taken = jnp.logical_and(host_ref[h] == ex, source_ref[h] == i)
                total = total + jnp.where(taken, CE[i], 0.0)
        summed = jnp.sum(jnp.sum(total, axis=0, keepdims=True), axis=1, keepdims=True)
        load_ref[...] = summed.astype(jnp.int32)

    def x_stage(c):
        width = CHUNKS[c][1] - CHUNKS[c][0]
        for d in OFFS:
            arrived(("sib", c, d), block(c, d, core=1 - k))
        picked = jnp.dot(OH[...], T[c][...].reshape(NSRC * tok_rows, width), preferred_element_type=F32)
        G[c][...] = picked.astype(BF16).reshape(NX, 2, UNIT, width)
        for j in (2, 1, 3):
            xp = xat(j)
            send(("x", c, j), G[c].at[xp], XY[c].at[pl.ds(0, 2), x], device(xp, y, z, k))
        XY[c][0, x] = G[c][x, 0]
        XY[c][1, x] = G[c][x, 1]

    def y_stage(c):
        for j in (1, 3, 2):
            arrived(("x", c, j), XY[c].at[pl.ds(0, 2), xat(-j)])
        for j in (1, 3, 2):
            a = lax.rem(p + j, 2)
            send(("y", c, j), XY[c].at[a], XY[c].at[1 + j], device(x, yat(j), z, k))

    def load_weights():
        load_in.wait()
        load_down.wait()

        def one(i, carry):
            rows = pl.ds(pl.multiple_of(i * 160, 16), 160)
            WU[rows, :] = WI[rows, ff:2 * ff]
            return carry
        lax.fori_loop(0, WI.shape[0] // 160, one, 0)

    def expert(j):
        slot = p if j == 0 else 1 + j
        gate = up = None
        for c, (lo, hi) in enumerate(CHUNKS):
            if j:
                arrived(("y", c, j), XY[c].at[slot])
            rows = XY[c][slot].reshape(NX * UNIT, hi - lo)
            g = jnp.dot(rows, WI[lo:hi, 0:ff], preferred_element_type=F32)
            u = jnp.dot(rows, WU[lo:hi, :], preferred_element_type=F32)
            gate, up = (g, u) if gate is None else (gate + g, up + u)
        HID[j * NX * UNIT:(j + 1) * NX * UNIT, :] = ((up + 1.0) * gate * jax.nn.sigmoid(1.702 * gate)).astype(BF16)

    def down(c):
        lo, hi = CHUNKS[c]
        part = jnp.dot(HID[...], WD[:, lo:hi], preferred_element_type=F32).astype(BF16)
        PP[c][...] = part.reshape(NY, NX, UNIT, hi - lo)
        for j in (1, 3, 2):
            send(("ry", c, j), PP[c].at[j], RY[c].at[j - 1], device(x, yat(-j), z, k))

    def halves(c):
        for j in (1, 3, 2):
            arrived(("ry", c, j), RY[c].at[j - 1])

        def one(i, carry):
            SS[c][p, i] = (PP[c][0, i].astype(F32) + RY[c][1, i].astype(F32)).astype(BF16)
            SS[c][1 - p, i] = (RY[c][0, i].astype(F32) + RY[c][2, i].astype(F32)).astype(BF16)
            return carry
        lax.fori_loop(0, NX, one, 0)
        for j in (2, 1, 3):
            xs = xat(j)
            send(("rx", c, j), SS[c].at[pl.ds(0, 2), xs], RX[c].at[x], device(xs, y, z, k))
        RX[c][x, 0] = SS[c][0, x]
        RX[c][x, 1] = SS[c][1, x]

    def combine(c):
        lo, hi = CHUNKS[c]
        for j in (2, 1, 3):
            arrived(("rx", c, j), RX[c].at[xat(-j)])

        def all_rows(core):
            rows = CT[pl.ds(pl.multiple_of(core * NZ * tok_rows, tok_rows), NZ * tok_rows), :]
            total = jnp.dot(rows, RX[c][...].reshape(ROWS, hi - lo), preferred_element_type=F32)
            return total.reshape(NZ, tok_rows, hi - lo)
        other = pl.ds((1 - k) * NZ, NZ)
        T[c][other] = all_rows(1 - k).astype(BF16)
        send(("zc", c), T[c].at[other], ZC[c], device(x, y, z, 1 - k))
        OWN[c][...] = all_rows(k)

    def scatter_step(c, s):
        lo, hi = CHUNKS[c]
        if s == 0:
            arrived(("zc", c), ZC[c])

        def partial(d, rows=slice(None)):
            return OWN[c][zat(d), rows] + ZC[c][zat(d), rows].astype(F32)

        if s == 0:
            own = T[c].at[k * NZ + zat(4)]
            own[...] = partial(4).astype(BF16)
            for i, way in enumerate((1, -1)):
                rows = pl.ds(i * half, half)
                send(("rs", c, 0, way), own.at[rows], ZR[c].at[i * 4, rows], device(x, y, zat(way), k))
        elif s < 4:
            for i, way in enumerate((1, -1)):
                d = way * (4 - s)
                own = T[c].at[k * NZ + zat(d)]
                if s == 1:
                    rows = pl.ds(i * half, half)
                    rest = pl.ds((1 - i) * half, half)
                    own[rest, :] = partial(d, rest).astype(BF16)
                    arrived(("rs", c, 0, way), ZR[c].at[i * 4, rows])
                    own[rows, :] = (partial(d, rows) + ZR[c][i * 4, rows].astype(F32)).astype(BF16)
                else:
                    arrived(("rs", c, s - 1, way), ZR[c].at[i * 4 + s - 1])
                    own[...] = (partial(d) + ZR[c][i * 4 + s - 1].astype(F32)).astype(BF16)
                send(("rs", c, s, way), own, ZR[c].at[i * 4 + s], device(x, y, zat(way), k))
        else:
            total = partial(0)
            for i, way in enumerate((1, -1)):
                arrived(("rs", c, 3, way), ZR[c].at[i * 4 + 3])
                total = total + ZR[c][i * 4 + 3].astype(F32)
            out_ref[lo:hi, :] = total.T.astype(BF16)

    gather_step(0, 1)
    make_meta()
    send_meta()
    waiting = []
    for t in range(2, 6 + max(BEGIN)):
        for c in OUTWARD:
            if 1 <= t - BEGIN[c] <= 5:
                gather_step(c, t - BEGIN[c])
        if t == 3:
            build_pick()
        while waiting:
            y_stage(waiting.pop(0))
        for c in OUTWARD:
            if t - BEGIN[c] == 5:
                x_stage(c)
                waiting.append(c)
                if c == OUTWARD[0]:
                    count_pairs()
                    load_weights()
                if c == OUTWARD[2]:
                    count_along_y()
    y_stage(waiting.pop(0))
    count_upper()
    expert(0)
    build_combine()
    drain()
    spread_upper()
    for j in (1, 3, 2):
        expert(j)
    down(BACK[0])
    down(BACK[1])
    halves(BACK[0])
    down(BACK[2])
    combine(BACK[0])
    scatter_step(BACK[0], 0)
    halves(BACK[1])
    down(BACK[3])
    finish_load()
    scatter_step(BACK[0], 1)
    combine(BACK[1])
    scatter_step(BACK[1], 0)
    scatter_step(BACK[0], 2)
    halves(BACK[2])
    scatter_step(BACK[1], 1)
    scatter_step(BACK[0], 3)
    combine(BACK[2])
    scatter_step(BACK[2], 0)
    scatter_step(BACK[1], 2)
    scatter_step(BACK[0], 4)
    halves(BACK[3])
    scatter_step(BACK[2], 1)
    scatter_step(BACK[1], 3)
    combine(BACK[3])
    scatter_step(BACK[3], 0)
    scatter_step(BACK[2], 2)
    scatter_step(BACK[3], 1)
    scatter_step(BACK[1], 4)
    scatter_step(BACK[2], 3)
    scatter_step(BACK[3], 2)
    scatter_step(BACK[2], 4)
    scatter_step(BACK[3], 3)
    scatter_step(BACK[3], 4)
    drain()

    def end_one(j, carry):
        meta_copy(j).wait_send()
        return carry
    lax.fori_loop(1, NSRC, end_one, 0)
    assert len(ids_of) <= send_sems.shape[0]


def moe(ids, weights, tokens, source, host, w_in, w_down):
    model, rows = tokens.shape
    widths = [hi - lo for lo, hi in CHUNKS]
    lead = (
        (NSRC, rows), (NX, 2, UNIT), (5, NX, UNIT), (4, NX, UNIT), (3, NX, UNIT), (2, NX, UNIT), (NX, 2, UNIT),
        (NZ, rows), (8, rows))
    buffers = [pltpu.VMEM(shape + (width,), BF16) for shape in lead for width in widths]
    buffers += [pltpu.VMEM((NZ, rows, width), F32) for width in widths]
    copies = NC * (8 + 8 + 3 + 3 + 3 + 3 + 1 + 8) + 3 + 3 + 3 + 12
    vmem = pl.BlockSpec(memory_space=pltpu.VMEM)
    smem = pl.BlockSpec(memory_space=pltpu.SMEM)
    hbm = pl.BlockSpec(memory_space=pl.ANY)
    return pl.pallas_call(
        moe_kernel,
        out_shape=(jax.ShapeDtypeStruct((model, rows), BF16), jax.ShapeDtypeStruct((1, 1), jnp.int32)),
        in_specs=[vmem, vmem, vmem, smem, smem, hbm, hbm],
        out_specs=(vmem, vmem),
        scratch_shapes=buffers + [
            pltpu.VMEM((NSRC, 8, 128), F32),
            pltpu.VMEM((ROWS, NSRC * rows), BF16),
            pltpu.VMEM((NSRC * rows, ROWS), BF16),
            pltpu.VMEM(w_in.shape, BF16),
            pltpu.VMEM((w_in.shape[0], w_down.shape[0]), BF16),
            pltpu.VMEM(w_down.shape, BF16),
            pltpu.VMEM((NY * NX * UNIT, w_down.shape[0]), BF16),
            pltpu.VMEM((NX, 8, 128), F32),
            pltpu.VMEM((NY, 8, 128), F32),
            pltpu.VMEM((NSRC + 1, 8, 128), F32),
            pltpu.SemaphoreType.DMA((copies,)),
            pltpu.SemaphoreType.DMA((copies,)),
            pltpu.SemaphoreType.DMA((NSRC,)),
            pltpu.SemaphoreType.DMA((NSRC,)),
            pltpu.SemaphoreType.DMA((2,)),
        ],
        compiler_params=pltpu.CompilerParams(
            collective_id=0, has_side_effects=True, vmem_limit_bytes=60 * 1024 * 1024),
        cost_estimate=pl.CostEstimate(flops=16 * 10**9, bytes_accessed=7 * 10**6, transcendentals=10**6),
    )(ids, weights, tokens, source, host, w_in, w_down)


def local(tokens, expert_ids, route_weights, w_in, w_down, spare_source, spare_host):
    mixed, slot_load = moe(expert_ids.T, route_weights.T, tokens.T, spare_source, spare_host, w_in[0, 0], w_down[0, 0])
    return mixed.T, slot_load


def solution(mesh):
    placed = (
        P(("rep", "exp"), None),
        P(("rep", "exp"), None),
        P(("rep", "exp"), None),
        P("rep", "exp", None, None),
        P("rep", "exp", None, None),
        P(),
        P(),
    )
    return jax.shard_map(
        local,
        mesh=mesh,
        in_specs=placed,
        out_specs=(P(("rep", "exp"), None), P("rep", "exp")),
        check_vma=False,
    )
```

```python
import jax
import jax.numpy as jnp
from jax import lax
from jax.experimental import pallas as pl
from jax.experimental.pallas import tpu as pltpu
from jax.sharding import PartitionSpec as P

MESH = pl.DeviceIdType.MESH
F32 = jnp.float32
BF16 = jnp.bfloat16

NX, NY, NZ = 4, 4, 8
NSRC = 2 * NZ
CAP = 5
UNIT = NSRC * CAP
ROWS = NX * 2 * UNIT
CODE = 1024
CHUNKS = ((0, 256), (256, 768), (768, 1280), (1280, 1440))
BEGIN = (0, 2, 3, 1)
OUTWARD = (0, 3, 1, 2)
BACK = (0, 1, 2, 3)
NC = len(CHUNKS)
OFFS = (0, -1, 1, -2, 2, -3, 3, 4)


def device(x, y, z, k):
    return (y * 4 + lax.rem(z, 2) * 2 + k, x * 4 + lax.div(z, 2))


def moe_kernel(ids_ref, wts_ref, tok_ref, source_ref, host_ref, wi_hbm, wd_hbm, out_ref, load_ref, *scratch):
    T, G, XY, PP, RY, SS, RX, ZC, ZR, OWN = (scratch[i * NC:(i + 1) * NC] for i in range(10))
    meta, OH, CT, WI, WU, WD, HID, ACC, CX, CY, CE, send_sems, recv_sems, meta_send, meta_recv, load_sems = scratch[10 * NC:]
    tok_rows = tok_ref.shape[1]
    half = tok_rows // 2
    ff = WD.shape[0]

    rep, ex = lax.axis_index("rep"), lax.axis_index("exp")
    y, k = lax.div(rep, 4), lax.rem(rep, 2)
    x = lax.div(ex, 4)
    z = lax.rem(ex, 4) * 2 + lax.rem(lax.div(rep, 2), 2)
    me = k * NZ + z
    p = lax.rem(y, 2)

    def zat(d):
        return lax.rem(z + d + NZ, NZ)

    def yat(d):
        return lax.rem(y + d + NY, NY)

    def xat(d):
        return lax.rem(x + d + NX, NX)

    ids_of = {}
    sends = []

    def sem_of(name):
        if name not in ids_of:
            ids_of[name] = len(ids_of)
        return ids_of[name]

    def send(name, src, dst, to):
        i = sem_of(name)
        copy = pltpu.make_async_remote_copy(
            src_ref=src, dst_ref=dst, send_sem=send_sems.at[i], recv_sem=recv_sems.at[i],
            device_id=to, device_id_type=MESH)
        copy.start()
        sends.append(copy)

    def arrived(name, dst):
        i = sem_of(name)
        pltpu.make_async_remote_copy(
            src_ref=dst, dst_ref=dst, send_sem=send_sems.at[i], recv_sem=recv_sems.at[i],
            device_id=device(x, y, z, 1 - k), device_id_type=MESH).wait_recv()

    def drain():
        for copy in sends:
            copy.wait_send()
        sends.clear()

    barrier = pltpu.get_barrier_semaphore()
    for j in range(1, NSRC):
        peer = lax.rem(me + j, NSRC)
        pl.semaphore_signal(barrier, inc=1, device_id=device(x, y, lax.rem(peer, NZ), lax.div(peer, NZ)), device_id_type=MESH)
    for j in range(1, NX):
        pl.semaphore_signal(barrier, inc=1, device_id=device(xat(j), y, z, k), device_id_type=MESH)
    for j in range(1, NY):
        pl.semaphore_signal(barrier, inc=1, device_id=device(x, yat(j), z, k), device_id_type=MESH)

    load_in = pltpu.make_async_copy(wi_hbm, WI, load_sems.at[0])
    load_down = pltpu.make_async_copy(wd_hbm, WD, load_sems.at[1])
    load_in.start()
    load_down.start()
    for c, (lo, hi) in enumerate(CHUNKS):
        T[c][me] = tok_ref[lo:hi, :].T
    pl.semaphore_wait(barrier, NSRC - 1 + NX - 1 + NY - 1)

    def block(c, d, rows=None, core=None):
        ref = T[c].at[(k if core is None else core) * NZ + zat(d)]
        return ref if rows is None else ref.at[pl.ds(rows, half)]

    def to_sibling(c, d):
        send(("sib", c, d), block(c, d), block(c, d), device(x, y, z, 1 - k))

    def gather_step(c, s):
        if s == 1:
            to_send = ((1, block(c, 0)), (-1, block(c, 0)))
        else:
            for way in (1, -1):
                rows = None if s <= 4 else (0 if way == 1 else half)
                arrived(("ag", c, s - 1, way), block(c, -(s - 1) * way, rows))
            to_send = ()
            if s <= 4:
                to_send = tuple(
                    (way, block(c, -(s - 1) * way, None if s < 4 else (0 if way == 1 else half))) for way in (1, -1))
        for way, ref in to_send:
            send(("ag", c, s, way), ref, ref, device(x, y, zat(way), k))
        if s == 1:
            to_sibling(c, 0)
        elif s <= 4:
            to_sibling(c, -(s - 1))
            to_sibling(c, s - 1)
        else:
            to_sibling(c, 4)

    def make_meta():
        experts = lax.broadcasted_iota(jnp.int32, (128, tok_rows), 0)
        hits = [(ids_ref[i:i + 1, :] == experts).astype(F32) for i in range(4)]
        total = hits[0] + hits[1] + hits[2] + hits[3]
        before = (lax.broadcasted_iota(jnp.int32, (tok_rows, tok_rows), 0)
                  < lax.broadcasted_iota(jnp.int32, (tok_rows, tok_rows), 1)).astype(F32).astype(BF16)
        earlier = jnp.dot(total.astype(BF16), before, preferred_element_type=F32)
        for i in range(4):
            rank = jnp.sum(earlier * hits[i], axis=0, keepdims=True)
            e = ids_ref[i:i + 1, :]
            owner = (e & 1) * NZ + ((e >> 3) & 3) * 2 + ((e >> 1) & 1)
            place = ((e >> 5) * 2 + ((e >> 2) & 1)) * UNIT
            meta[me, i:i + 1, :] = (owner * CODE + place).astype(F32) + rank
            meta[me, 4 + i:5 + i, :] = wts_ref[i:i + 1, :]

    def send_meta():
        def one(j, carry):
            peer = lax.rem(me + j, NSRC)
            pltpu.make_async_remote_copy(
                src_ref=meta.at[me], dst_ref=meta.at[me], send_sem=meta_send.at[j], recv_sem=meta_recv.at[j],
                device_id=device(x, y, lax.rem(peer, NZ), lax.div(peer, NZ)), device_id_type=MESH).start()
            return carry
        lax.fori_loop(1, NSRC, one, 0)

    def meta_copy(j):
        peer = lax.rem(me + NSRC - j, NSRC)
        return pltpu.make_async_remote_copy(
            src_ref=meta.at[peer], dst_ref=meta.at[peer], send_sem=meta_send.at[j], recv_sem=meta_recv.at[j],
            device_id=device(x, y, lax.rem(peer, NZ), lax.div(peer, NZ)), device_id_type=MESH)

    def build_pick():
        def wait_one(j, carry):
            meta_copy(j).wait_recv()
            return carry
        lax.fori_loop(1, NSRC, wait_one, 0)

        def one(s, carry):
            row = lax.broadcasted_iota(jnp.int32, (ROWS, tok_rows), 0).astype(F32)
            shift = (s * CAP - me * CODE).astype(F32)
            codes = meta[s] + shift
            hit = row == codes[0:1, :]
            for i in range(1, 4):
                hit = jnp.logical_or(hit, row == codes[i:i + 1, :])
            OH[:, pl.ds(pl.multiple_of(s * tok_rows, tok_rows), tok_rows)] = jnp.where(hit, 1.0, 0.0).astype(BF16)
            return carry
        lax.fori_loop(0, NSRC, one, 0)

    def build_combine():
        def one(s, carry):
            col = lax.broadcasted_iota(jnp.int32, (tok_rows, ROWS), 1).astype(F32)
            shift = (s * CAP - me * CODE).astype(F32)
            info = meta[s].T
            total = jnp.zeros((tok_rows, ROWS), F32)
            for i in range(4):
                total = jnp.where(col == info[:, i:i + 1] + shift, info[:, 4 + i:5 + i], total)
            CT[pl.ds(pl.multiple_of(s * tok_rows, tok_rows), tok_rows), :] = total.astype(BF16)
            return carry
        lax.fori_loop(0, NSRC, one, 0)

    def count_pairs():
        codes = meta[...] - (me * CODE).astype(F32)
        valid = lax.broadcasted_iota(jnp.int32, codes.shape, 1) < 4
        unit = lax.broadcasted_iota(jnp.int32, (8, 128), 0)
        table = jnp.zeros((8, 128), F32)
        for u in range(2 * NX):
            inside = jnp.logical_and(valid, jnp.logical_and(codes >= u * UNIT, codes < (u + 1) * UNIT))
            hits = jnp.sum(jnp.sum(jnp.where(inside, 1.0, 0.0), axis=0), axis=0, keepdims=True)
            table = jnp.where(unit == u, hits, table)
        CX[x] = table
        for j in range(1, NX):
            send(("cx", j), CX.at[x], CX.at[x], device(xat(j), y, z, k))

    def count_along_y():
        for j in range(1, NX):
            arrived(("cx", j), CX.at[xat(-j)])
        CY[y] = CX[0] + CX[1] + CX[2] + CX[3]
        for j in range(1, NY):
            send(("cy", j), CY.at[y], CY.at[y], device(x, yat(j), z, k))

    def count_upper():
        for j in range(1, NY):
            arrived(("cy", j), CY.at[yat(-j)])
        mine = lax.broadcasted_iota(jnp.int32, (8, 128), 0) == x * 2 + p
        CE[NSRC] = jnp.where(mine, CY[0] + CY[1], 0.0)
        CE[ex] = jnp.where(mine, CY[2] + CY[3], 0.0)
        for j in range(1, NX):
            send(("ce", j), CE.at[ex], CE.at[ex], device(xat(j), y, z, k))

    def column(i, j):
        return i * 4 + lax.div(zat(NZ - 2 * j), 2)

    def spread_upper():
        for j in range(1, NX):
            arrived(("ce", j), CE.at[xat(-j) * 4 + lax.div(z, 2)])
        for j in range(1, NZ // 2):
            for i in range(NX):
                send(("cz", i, j), CE.at[column(i, 0)], CE.at[column(i, 0)], device(x, y, zat(2 * j), k))

    def finish_load():
        for j in range(1, NZ // 2):
            for i in range(NX):
                arrived(("cz", i, j), CE.at[column(i, j)])
        total = CE[NSRC]
        upper = CE[ex]
        for h in range(source_ref.shape[0]):
            upper = jnp.where(source_ref[h] == ex, 0.0, upper)
        total = total + upper
        for h in range(source_ref.shape[0]):
            for i in range(NSRC):
                taken = jnp.logical_and(host_ref[h] == ex, source_ref[h] == i)
                total = total + jnp.where(taken, CE[i], 0.0)
        summed = jnp.sum(jnp.sum(total, axis=0, keepdims=True), axis=1, keepdims=True)
        load_ref[...] = summed.astype(jnp.int32)

    def x_stage(c):
        width = CHUNKS[c][1] - CHUNKS[c][0]
        for d in OFFS:
            arrived(("sib", c, d), block(c, d, core=1 - k))
        picked = jnp.dot(OH[...], T[c][...].reshape(NSRC * tok_rows, width), preferred_element_type=F32)
        G[c][...] = picked.astype(BF16).reshape(NX, 2, UNIT, width)
        for j in (2, 1, 3):
            xp = xat(j)
            send(("x", c, j), G[c].at[xp], XY[c].at[pl.ds(0, 2), x], device(xp, y, z, k))
        XY[c][0, x] = G[c][x, 0]
        XY[c][1, x] = G[c][x, 1]

    def y_stage(c):
        for j in (1, 3, 2):
            arrived(("x", c, j), XY[c].at[pl.ds(0, 2), xat(-j)])
        for j in (1, 3, 2):
            a = lax.rem(p + j, 2)
            send(("y", c, j), XY[c].at[a], XY[c].at[1 + j], device(x, yat(j), z, k))

    def load_weights():
        load_in.wait()
        load_down.wait()

        def one(i, carry):
            rows = pl.ds(pl.multiple_of(i * 160, 16), 160)
            WU[rows, :] = WI[rows, ff:2 * ff]
            return carry
        lax.fori_loop(0, WI.shape[0] // 160, one, 0)

    def expert(j, chunks, first, last):
        slot = p if j == 0 else 1 + j
        gate, up = (None, None) if first else (ACC[j - 1, :, 0:ff], ACC[j - 1, :, 768:768 + ff])
        for c in chunks:
            lo, hi = CHUNKS[c]
            if j:
                arrived(("y", c, j), XY[c].at[slot])
            rows = XY[c][slot].reshape(NX * UNIT, hi - lo)
            g = jnp.dot(rows, WI[lo:hi, 0:ff], preferred_element_type=F32)
            u = jnp.dot(rows, WU[lo:hi, :], preferred_element_type=F32)
            gate, up = (g, u) if gate is None else (gate + g, up + u)
        if last:
            HID[j * NX * UNIT:(j + 1) * NX * UNIT, :] = ((up + 1.0) * gate * jax.nn.sigmoid(1.702 * gate)).astype(BF16)
        else:
            ACC[j - 1, :, 0:ff] = gate
            ACC[j - 1, :, 768:768 + ff] = up

    def down(c):
        lo, hi = CHUNKS[c]
        part = jnp.dot(HID[...], WD[:, lo:hi], preferred_element_type=F32).astype(BF16)
        PP[c][...] = part.reshape(NY, NX, UNIT, hi - lo)
        for j in (1, 3, 2):
            send(("ry", c, j), PP[c].at[j], RY[c].at[j - 1], device(x, yat(-j), z, k))

    def halves(c):
        for j in (1, 3, 2):
            arrived(("ry", c, j), RY[c].at[j - 1])

        def one(i, carry):
            SS[c][p, i] = (PP[c][0, i].astype(F32) + RY[c][1, i].astype(F32)).astype(BF16)
            SS[c][1 - p, i] = (RY[c][0, i].astype(F32) + RY[c][2, i].astype(F32)).astype(BF16)
            return carry
        lax.fori_loop(0, NX, one, 0)
        for j in (2, 1, 3):
            xs = xat(j)
            send(("rx", c, j), SS[c].at[pl.ds(0, 2), xs], RX[c].at[x], device(xs, y, z, k))
        RX[c][x, 0] = SS[c][0, x]
        RX[c][x, 1] = SS[c][1, x]

    def combine(c):
        lo, hi = CHUNKS[c]
        for j in (2, 1, 3):
            arrived(("rx", c, j), RX[c].at[xat(-j)])

        def all_rows(core):
            rows = CT[pl.ds(pl.multiple_of(core * NZ * tok_rows, tok_rows), NZ * tok_rows), :]
            total = jnp.dot(rows, RX[c][...].reshape(ROWS, hi - lo), preferred_element_type=F32)
            return total.reshape(NZ, tok_rows, hi - lo)
        other = pl.ds((1 - k) * NZ, NZ)
        T[c][other] = all_rows(1 - k).astype(BF16)
        send(("zc", c), T[c].at[other], ZC[c], device(x, y, z, 1 - k))
        OWN[c][...] = all_rows(k)

    def scatter_step(c, s):
        lo, hi = CHUNKS[c]
        if s == 0:
            arrived(("zc", c), ZC[c])

        def partial(d, rows=slice(None)):
            return OWN[c][zat(d), rows] + ZC[c][zat(d), rows].astype(F32)

        if s == 0:
            own = T[c].at[k * NZ + zat(4)]
            own[...] = partial(4).astype(BF16)
            for i, way in enumerate((1, -1)):
                rows = pl.ds(i * half, half)
                send(("rs", c, 0, way), own.at[rows], ZR[c].at[i * 4, rows], device(x, y, zat(way), k))
        elif s < 4:
            for i, way in enumerate((1, -1)):
                d = way * (4 - s)
                own = T[c].at[k * NZ + zat(d)]
                if s == 1:
                    rows = pl.ds(i * half, half)
                    rest = pl.ds((1 - i) * half, half)
                    own[rest, :] = partial(d, rest).astype(BF16)
                    arrived(("rs", c, 0, way), ZR[c].at[i * 4, rows])
                    own[rows, :] = (partial(d, rows) + ZR[c][i * 4, rows].astype(F32)).astype(BF16)
                else:
                    arrived(("rs", c, s - 1, way), ZR[c].at[i * 4 + s - 1])
                    own[...] = (partial(d) + ZR[c][i * 4 + s - 1].astype(F32)).astype(BF16)
                send(("rs", c, s, way), own, ZR[c].at[i * 4 + s], device(x, y, zat(way), k))
        else:
            total = partial(0)
            for i, way in enumerate((1, -1)):
                arrived(("rs", c, 3, way), ZR[c].at[i * 4 + 3])
                total = total + ZR[c][i * 4 + 3].astype(F32)
            out_ref[lo:hi, :] = total.T.astype(BF16)

    gather_step(0, 1)
    make_meta()
    send_meta()
    waiting = []
    for t in range(2, 6 + max(BEGIN)):
        for c in OUTWARD:
            if 1 <= t - BEGIN[c] <= 5:
                gather_step(c, t - BEGIN[c])
        if t == 3:
            build_pick()
        while waiting:
            y_stage(waiting.pop(0))
        for c in OUTWARD:
            if t - BEGIN[c] == 5:
                x_stage(c)
                waiting.append(c)
                if c == OUTWARD[0]:
                    count_pairs()
                    load_weights()
                if c == OUTWARD[2]:
                    count_along_y()
    y_stage(waiting.pop(0))
    count_upper()
    expert(0, OUTWARD, True, True)
    build_combine()
    drain()
    spread_upper()
    for j in (1, 3, 2):
        expert(j, OUTWARD[:-1], True, False)
    for j in (1, 3, 2):
        expert(j, OUTWARD[-1:], False, True)
    down(BACK[0])
    down(BACK[1])
    halves(BACK[0])
    down(BACK[2])
    combine(BACK[0])
    scatter_step(BACK[0], 0)
    halves(BACK[1])
    down(BACK[3])
    finish_load()
    scatter_step(BACK[0], 1)
    combine(BACK[1])
    scatter_step(BACK[1], 0)
    scatter_step(BACK[0], 2)
    halves(BACK[2])
    scatter_step(BACK[1], 1)
    scatter_step(BACK[0], 3)
    combine(BACK[2])
    scatter_step(BACK[2], 0)
    scatter_step(BACK[1], 2)
    scatter_step(BACK[0], 4)
    halves(BACK[3])
    scatter_step(BACK[2], 1)
    scatter_step(BACK[1], 3)
    combine(BACK[3])
    scatter_step(BACK[3], 0)
    scatter_step(BACK[2], 2)
    scatter_step(BACK[3], 1)
    scatter_step(BACK[1], 4)
    scatter_step(BACK[2], 3)
    scatter_step(BACK[3], 2)
    scatter_step(BACK[2], 4)
    scatter_step(BACK[3], 3)
    scatter_step(BACK[3], 4)
    drain()

    def end_one(j, carry):
        meta_copy(j).wait_send()
        return carry
    lax.fori_loop(1, NSRC, end_one, 0)
    assert len(ids_of) <= send_sems.shape[0]


def moe(ids, weights, tokens, source, host, w_in, w_down):
    model, rows = tokens.shape
    widths = [hi - lo for lo, hi in CHUNKS]
    lead = (
        (NSRC, rows), (NX, 2, UNIT), (5, NX, UNIT), (4, NX, UNIT), (3, NX, UNIT), (2, NX, UNIT), (NX, 2, UNIT),
        (NZ, rows), (8, rows))
    buffers = [pltpu.VMEM(shape + (width,), BF16) for shape in lead for width in widths]
    buffers += [pltpu.VMEM((NZ, rows, width), F32) for width in widths]
    copies = NC * (8 + 8 + 3 + 3 + 3 + 3 + 1 + 8) + 3 + 3 + 3 + 12
    vmem = pl.BlockSpec(memory_space=pltpu.VMEM)
    smem = pl.BlockSpec(memory_space=pltpu.SMEM)
    hbm = pl.BlockSpec(memory_space=pl.ANY)
    return pl.pallas_call(
        moe_kernel,
        out_shape=(jax.ShapeDtypeStruct((model, rows), BF16), jax.ShapeDtypeStruct((1, 1), jnp.int32)),
        in_specs=[vmem, vmem, vmem, smem, smem, hbm, hbm],
        out_specs=(vmem, vmem),
        scratch_shapes=buffers + [
            pltpu.VMEM((NSRC, 8, 128), F32),
            pltpu.VMEM((ROWS, NSRC * rows), BF16),
            pltpu.VMEM((NSRC * rows, ROWS), BF16),
            pltpu.VMEM(w_in.shape, BF16),
            pltpu.VMEM((w_in.shape[0], w_down.shape[0]), BF16),
            pltpu.VMEM(w_down.shape, BF16),
            pltpu.VMEM((NY * NX * UNIT, w_down.shape[0]), BF16),
            pltpu.VMEM((NY - 1, NX * UNIT, 1536), F32),
            pltpu.VMEM((NX, 8, 128), F32),
            pltpu.VMEM((NY, 8, 128), F32),
            pltpu.VMEM((NSRC + 1, 8, 128), F32),
            pltpu.SemaphoreType.DMA((copies,)),
            pltpu.SemaphoreType.DMA((copies,)),
            pltpu.SemaphoreType.DMA((NSRC,)),
            pltpu.SemaphoreType.DMA((NSRC,)),
            pltpu.SemaphoreType.DMA((2,)),
        ],
        compiler_params=pltpu.CompilerParams(
            collective_id=0, has_side_effects=True, vmem_limit_bytes=62 * 1024 * 1024),
        cost_estimate=pl.CostEstimate(flops=16 * 10**9, bytes_accessed=7 * 10**6, transcendentals=10**6),
    )(ids, weights, tokens, source, host, w_in, w_down)


def local(tokens, expert_ids, route_weights, w_in, w_down, spare_source, spare_host):
    mixed, slot_load = moe(expert_ids.T, route_weights.T, tokens.T, spare_source, spare_host, w_in[0, 0], w_down[0, 0])
    return mixed.T, slot_load


def solution(mesh):
    placed = (
        P(("rep", "exp"), None),
        P(("rep", "exp"), None),
        P(("rep", "exp"), None),
        P("rep", "exp", None, None),
        P("rep", "exp", None, None),
        P(),
        P(),
    )
    return jax.shard_map(
        local,
        mesh=mesh,
        in_specs=placed,
        out_specs=(P(("rep", "exp"), None), P("rep", "exp")),
        check_vma=False,
    )
```
